32 devices in a mesh: req: 16 (over z, y, core), tp: 2 (over x).
Axes of the slice: x: 2, y: 2, z: 4, core: 2. Of those that a mesh axis runs over, the one named last changes fastest.
Arguments:
- queries: bfloat16 [4096, 5120], P('req', 'tp')
- new_keys: bfloat16 [4096, 5120], P('req', 'tp')
- new_values: bfloat16 [4096, 5120], P('req', 'tp'), may hold values from -6 to 6
- query_gain: float32 [5120], P('tp'), may hold values from 0.1 to 1.9
- key_gain: float32 [5120], P('tp'), may hold values from 0.4 to 2.5
- cache_keys: bfloat16 [1024, 8, 5120], P('req', None, 'tp')
- cache_values: bfloat16 [1024, 8, 5120], P('req', None, 'tp'), may hold values from -6 to 6
- page_table: int32 [16, 48], P('req'), may hold values from 0 to 63, as said below
- cache_lens: int32 [16], P('req'), may hold values from 48 to 384, as said below
- mig_pages: int32 [16, 16], P('req'), may hold values from 0 to 63, as said below
- mig_dest: int32 [256, 1], P('req'), may hold values from 0 to 15; in each aligned block of 16 rows (0 to 15, 16 to 31, ...) at most 2 rows name the same one
- cross_queries: bfloat16 [4096, 5120], P('req', 'tp')
- text_keys: bfloat16 [2048, 5120], P('req', 'tp')
- text_values: bfloat16 [2048, 5120], P('req', 'tp'), may hold values from -6 to 6
- out_weight: bfloat16 [5120, 5120], P('tp', 'req'), may hold values from -0.5 to 0.5
- residual: bfloat16 [4096, 5120], P('req', 'tp')
- gate: bfloat16 [16, 5120], P('req', 'tp'), may hold values from -6 to 6
- shift: bfloat16 [16, 5120], P('req', 'tp'), may hold values from -3 to 3
- scale: bfloat16 [16, 5120], P('req', 'tp'), may hold values from -3 to 3
Outputs:
- stream: bfloat16 [4096, 5120], P('req', 'tp')
- normed: bfloat16 [4096, 5120], P('req', 'tp')
- cross_out: bfloat16 [4096, 5120], P('req', 'tp')
The draws below stay inside these ranges and needn't reach their ends.
Inputs may be any that keep to these rules, and one draw needn't show every extreme that they name: Row r of page_table and row r of mig_pages together name every one of the 64 pages of row r's pool exactly once. `mig_pages`: see page_table. `cache_lens`: at least 48; the largest is exactly 384. `mig_dest`: among the 16 pages of one request row (the rows of one device) no destination is named more than 2 times.
All inputs are finite; a program needn't handle non-finite values.
Results may differ from the reference program's by a relative error of at most 0.014.
Values may be sent and summed in bfloat16 or wider, within the bound.
No kernel may reach another device: no remote copies, remote signals or barrier semaphores. Data moves between devices by JAX's collectives and lax.ppermute only.
A program may use at most 128 MiB of HBM per device.

```python
import math
import jax
import jax.numpy as jnp
import numpy as np
from jax import lax

HEADS = 40
HD = 128
D = 5120
TOK_DEV = 256
TEXT = 128
MAXP = 48
PAGE = 8
CAP = 2
MIG = 16
POOL = 64
TOKENS = 4096
N_REQ = 16
N_TP = 2


def scaled_field(key, row_count, row_low, row_high, column_low, column_high):
    base = jax.random.normal(jax.random.fold_in(key, 1), (row_count, D), jnp.float32)
    row_scale = jnp.exp(jax.random.uniform(jax.random.fold_in(key, 2), (row_count, 1), jnp.float32, math.log(row_low), math.log(row_high)))
    column_scale = jnp.exp(jax.random.uniform(jax.random.fold_in(key, 3), (1, D), jnp.float32, math.log(column_low), math.log(column_high)))
    ramp = 1.0 + 2.0 * jnp.arange(D, dtype=jnp.float32)[None, :] / (D - 1)
    return base * row_scale * column_scale * ramp


def pool_order(key):
    row_keys = jax.random.split(jax.random.fold_in(key, 11), N_REQ)
    return jax.vmap(lambda row_key: jax.random.permutation(row_key, POOL))(row_keys).astype(jnp.int32)


def draw_queries(key, part):
    field = scaled_field(jax.random.fold_in(key, 40), TOKENS, 1.0, 10.0, 1.0, 10.0)
    return field.astype(jnp.bfloat16)


def draw_new_keys(key, part):
    field = scaled_field(jax.random.fold_in(key, 50), TOKENS, 1.0, 10.0, 1.0, 10.0)
    return field.astype(jnp.bfloat16)


def draw_cache_keys(key, part):
    field = 2.5 * jax.random.normal(jax.random.fold_in(key, 60), (N_REQ * POOL, PAGE, D), jnp.float32)
    return field.astype(jnp.bfloat16)


def draw_page_table(key, part):
    return pool_order(key)[:, :MAXP]


def draw_mig_pages(key, part):
    return pool_order(key)[:, MAXP:]


def draw_cache_lens(key, part):
    lens_key = jax.random.fold_in(key, 21)
    lengths = jax.random.randint(jax.random.fold_in(lens_key, 1), (N_REQ,), MAXP * PAGE // 8, MAXP * PAGE + 1)
    longest = jax.random.randint(jax.random.fold_in(lens_key, 2), (), 0, N_REQ)
    return jnp.where(jnp.arange(N_REQ) == longest, MAXP * PAGE, lengths).astype(jnp.int32)


def draw_cross_queries(key, part):
    field = jax.random.normal(jax.random.fold_in(key, 70), (TOKENS, D), jnp.float32)
    return field.astype(jnp.bfloat16)


def draw_text_keys(key, part):
    field = 2.5 * jax.random.normal(jax.random.fold_in(key, 80), (N_REQ * TEXT, D), jnp.float32)
    return field.astype(jnp.bfloat16)


def draw_residual(key, part):
    field = scaled_field(jax.random.fold_in(key, 90), TOKENS, 0.1, 1.0, 0.3, 3.0)
    return field.astype(jnp.bfloat16)


def raised(array, stream_key, source, target, parts, factor):
    owner, partner = [(jnp.arange(array.shape[dim]) // (array.shape[dim] // parts)).reshape([-1 if axis == dim else 1 for axis in range(array.ndim)]) for dim in (source, target)]
    chosen = jax.random.permutation(stream_key, parts)[partner]
    strong = (owner == chosen) | (owner == (partner + parts // 2) % parts)
    return jnp.where(strong, factor * array, array)


def shard_levels(stream_key, dims, cuts, smallest, high):
    factor_of, own = 1.0, jax.random.fold_in(stream_key, 6)
    for dim, parts in cuts:
        heights = jnp.exp(jax.random.uniform(jax.random.fold_in(own, dim), (parts,), jnp.float32, smallest / len(cuts), high / len(cuts)))
        factor_of = factor_of * jnp.repeat(heights, dims[dim] // parts).reshape([-1 if axis == dim else 1 for axis in range(len(dims))])
    return factor_of


def deal_out(stream_key, own, number, rows, count, top, bound, skew):
    sequence = jax.random.permutation(stream_key, count)
    heavy_load, ordinary = load_shares(count, rows * top, bound, skew, True), load_shares(count, rows * top, bound, skew, False)
    places = jnp.arange(count)

    def named(tallies, offset_by):
        used = int((tallies > 0).sum())
        fixed = max(1, used // 4)
        moved = fixed + (places - fixed + offset_by * (used - fixed)) % max(1, count - fixed)
        return jnp.zeros((count,), jnp.int32).at[sequence[jnp.where(places < fixed, places, moved)]].set(jnp.asarray(tallies, jnp.int32))

    tallies = jnp.where(number % 4 == 0, named(heavy_load, number // 4), named(ordinary, number - number // 4 - 1))
    mixed = jax.random.permutation(jax.random.fold_in(own, 3), count)
    giver, taker = mixed[0:count // 2 * 2:2], mixed[1:count // 2 * 2:2]
    slack = jnp.minimum(tallies[giver] - 1, bound - tallies[taker]) // 2
    slack = jnp.where((giver == sequence[0]) | (taker == sequence[0]) | (tallies[taker] == 0), 0, jnp.maximum(slack, 0))
    moved = jax.random.randint(jax.random.fold_in(own, 4), (count // 2,), 0, 1 << 20) % (slack + 1)
    tallies = tallies.at[giver].add(-moved).at[taker].add(moved)
    labels = jnp.searchsorted(jnp.cumsum(tallies), jnp.arange(rows * top), side="right").astype(jnp.int32)
    table = labels.reshape(top, rows).T
    table = table[jax.random.permutation(jax.random.fold_in(own, 1), rows)]
    offset_by = jax.random.randint(jax.random.fold_in(own, 2), (rows, 1), 0, top)
    return jnp.take_along_axis(table, (jnp.arange(top)[None, :] + offset_by) % top, axis=1)


def load_shares(number_of, total, reach, slope, full):
    portions = [(1 << 20) // math.isqrt(rank ** slope) + 1 for rank in range(1, number_of + 1)]
    largest = reach if full else min(reach, max(-(-total // number_of), total * portions[0] // sum(portions)))
    least = 1 if total - largest >= number_of - 1 else 0
    holding, surplus = [largest] + [least] * (number_of - 1), total - largest - least * (number_of - 1)
    while surplus > 0:
        movable = [i for i in range(1, number_of) if holding[i] < largest] or [i for i in range(1, number_of) if holding[i] < reach]
        pool, budget = sum([portions[i] for i in movable]), surplus
        for i in movable:
            extra = min(reach - holding[i], max(1, budget * portions[i] // pool), surplus)
            holding[i] = holding[i] + extra
            surplus = surplus - extra
    return np.array(holding)


def bell_draw(rng, shape, width, reach, cuts=(), held_as=jnp.bfloat16):
    result = width * jax.random.normal(rng, shape, jnp.float32)
    if cuts:
        result = result * shard_levels(rng, shape, cuts, -0.22, 0.18)
    return jnp.clip(result, -reach, reach).astype(held_as)


def bell_draw_with(stream_key, dims, spread, limit, pieces, heavy, kind=jnp.bfloat16):
    result = spread * jax.random.normal(stream_key, dims, jnp.float32)
    if pieces:
        result = result * shard_levels(stream_key, dims, pieces, -0.22, 0.18)
    return jnp.clip(raised(result, jax.random.fold_in(stream_key, 3), *heavy), -limit, limit).astype(kind)


def setup_inputs(seed: int = 0) -> dict:
    key_of = jax.random.split(jax.random.key(seed), 20)
    queries = draw_queries(jax.random.fold_in(key_of[19], 71), 0)
    new_keys = draw_new_keys(jax.random.fold_in(key_of[19], 71), 0)
    new_values = bell_draw(key_of[2], (TOKENS, D), 1.0, 6.0, ((0, 16), (1, 2)))
    query_gain = jnp.clip(1.0 + 0.18 * jax.random.normal(key_of[3], (D,), jnp.float32), 0.1, 1.9)
    key_gain = jnp.clip(jnp.exp(math.log(2.5) - 1.8325814 * jax.random.uniform(key_of[4], (D,), jnp.float32) ** shard_levels(key_of[4], (D,), ((0, 2),), -0.2, 0.2)), 0.4, 2.5)
    cache_keys = draw_cache_keys(jax.random.fold_in(key_of[19], 71), 0)
    cache_values = bell_draw(key_of[6], (N_REQ * POOL, PAGE, D), 1.0, 6.0, ((0, 16), (2, 2)))
    page_table = draw_page_table(jax.random.fold_in(key_of[19], 71), 0)
    cache_lens = draw_cache_lens(jax.random.fold_in(key_of[19], 71), 0)
    mig_pages = draw_mig_pages(jax.random.fold_in(key_of[19], 71), 0)
    mig_dest_keys = jax.random.split(jax.random.fold_in(key_of[10], 1), (N_REQ * MIG) // MIG)
    mig_dest_turns = jax.random.permutation(jax.random.fold_in(key_of[10], 3), (N_REQ * MIG) // MIG)
    mig_dest = jax.vmap(lambda own, number: deal_out(jax.random.fold_in(key_of[10], 2), own, number, MIG, N_REQ, 1, CAP, 2))(mig_dest_keys, mig_dest_turns).reshape((N_REQ * MIG, 1))
    cross_queries = draw_cross_queries(jax.random.fold_in(key_of[19], 71), 0)
    text_keys = draw_text_keys(jax.random.fold_in(key_of[19], 71), 0)
    text_values = bell_draw(key_of[13], (N_REQ * TEXT, D), 1.0, 6.0, ((0, 16), (1, 2)))
    out_weight = bell_draw_with(key_of[14], (D, D), (D // 16) ** -0.5, 0.5, ((0, 2), (1, 16)), (0, 1, 16, 2.0))
    residual = draw_residual(jax.random.fold_in(key_of[19], 71), 0)
    gate = bell_draw(key_of[16], (N_REQ, D), 1.5, 6.0, ((0, 16), (1, 2)))
    shift = bell_draw(key_of[17], (N_REQ, D), 0.5, 3.0, ((0, 16), (1, 2)))
    scale = bell_draw(key_of[18], (N_REQ, D), 0.5, 3.0, ((0, 16), (1, 2)))
    return {"queries": queries, "new_keys": new_keys, "new_values": new_values, "query_gain": query_gain, "key_gain": key_gain, "cache_keys": cache_keys, "cache_values": cache_values, "page_table": page_table, "cache_lens": cache_lens, "mig_pages": mig_pages, "mig_dest": mig_dest, "cross_queries": cross_queries, "text_keys": text_keys, "text_values": text_values, "out_weight": out_weight, "residual": residual, "gate": gate, "shift": shift, "scale": scale}


EPS = 1e-06

def rms_normed(values, gain):
    floats = values.astype(jnp.float32)
    mean_square = lax.optimization_barrier(jnp.mean(floats * floats, axis=1, keepdims=True))
    return (floats * lax.rsqrt(mean_square + EPS) * gain).astype(jnp.bfloat16)

def attend(query_rows, key_rows, value_rows, usable):
    row_count = query_rows.shape[0]
    query_heads = query_rows.astype(jnp.float32).reshape(row_count, HEADS, HD)
    key_heads = key_rows.astype(jnp.float32).reshape(key_rows.shape[0], HEADS, HD)
    value_heads = value_rows.astype(jnp.float32).reshape(value_rows.shape[0], HEADS, HD)
    scores = jnp.einsum('qhd,khd->hqk', query_heads, key_heads) * (1.0 / math.sqrt(HD))
    if usable is not None:
        scores = jnp.where(usable[None, None, :], scores, -jnp.inf)
    row_max = lax.optimization_barrier(jnp.max(scores, axis=2, keepdims=True))
    exponent = jnp.exp(scores - row_max)
    denominator = lax.optimization_barrier(jnp.sum(exponent, axis=2))
    weights = lax.optimization_barrier(exponent.astype(jnp.bfloat16)).astype(jnp.float32)
    mixed = jnp.einsum('hqk,khd->qhd', weights, value_heads)
    mixed = mixed / jnp.transpose(denominator)[:, :, None]
    return mixed.reshape(row_count, HEADS * HD).astype(jnp.bfloat16)

def reference(queries, new_keys, new_values, query_gain, key_gain, cache_keys, cache_values, page_table, cache_lens, mig_pages, mig_dest, cross_queries, text_keys, text_values, out_weight, residual, gate, shift, scale):
    query_normed = rms_normed(queries, query_gain)
    key_normed = rms_normed(new_keys, key_gain)
    destination = mig_dest[:, 0].reshape(N_REQ, MIG)
    slot_match = (destination[:, :, None] == jnp.arange(N_REQ, dtype=jnp.int32)[None, None, :]).astype(jnp.int32)
    position = lax.optimization_barrier(jnp.sum(jnp.cumsum(slot_match, axis=1) * slot_match, axis=2)) - 1
    sources = jnp.broadcast_to(jnp.arange(N_REQ, dtype=jnp.int32)[:, None], (N_REQ, MIG))
    global_page = sources * POOL + mig_pages
    arrivals = jnp.full((N_REQ, N_REQ, CAP), -1, jnp.int32).at[destination, sources, position].set(global_page)

    def one_request(request):
        first = request * TOK_DEV
        query_rows = lax.dynamic_slice_in_dim(query_normed, first, TOK_DEV, 0)
        own_keys = lax.dynamic_slice_in_dim(key_normed, first, TOK_DEV, 0)
        own_values = lax.dynamic_slice_in_dim(new_values, first, TOK_DEV, 0)
        own_pages = request * POOL + page_table[request]
        resident_keys = cache_keys[own_pages].reshape(MAXP * PAGE, D)
        resident_values = cache_values[own_pages].reshape(MAXP * PAGE, D)
        resident_usable = jnp.arange(MAXP * PAGE, dtype=jnp.int32) < cache_lens[request]
        incoming = arrivals[request].reshape(-1)
        incoming_usable = jnp.repeat(incoming >= 0, PAGE)
        safe_pages = jnp.maximum(incoming, 0)
        arrived_keys = cache_keys[safe_pages].reshape(-1, D)
        arrived_values = cache_values[safe_pages].reshape(-1, D)
        all_keys = jnp.concatenate([resident_keys, arrived_keys, own_keys], axis=0)
        all_values = jnp.concatenate([resident_values, arrived_values, own_values], axis=0)
        usable = jnp.concatenate([resident_usable, incoming_usable, jnp.ones((TOK_DEV,), bool)])
        attended = attend(query_rows, all_keys, all_values, usable)
        cross_rows = lax.dynamic_slice_in_dim(cross_queries, first, TOK_DEV, 0)
        text_rows = lax.dynamic_slice_in_dim(text_keys, request * TEXT, TEXT, 0)
        text_vals = lax.dynamic_slice_in_dim(text_values, request * TEXT, TEXT, 0)
        crossed = attend(cross_rows, text_rows, text_vals, None)
        return (attended, crossed)
    attended, crossed = lax.map(one_request, jnp.arange(N_REQ, dtype=jnp.int32))
    attended = attended.reshape(TOKENS, D)
    cross_out = crossed.reshape(TOKENS, D)
    group_width = D // N_TP
    projected = jnp.zeros((TOKENS, D), jnp.float32)
    for group in range(N_TP):
        lower = group * group_width
        partial_term = jnp.dot(attended[:, lower:lower + group_width], out_weight[lower:lower + group_width, :], preferred_element_type=jnp.float32)
        projected = projected + lax.optimization_barrier(partial_term.astype(jnp.bfloat16)).astype(jnp.float32)
    gate_rows = jnp.repeat(gate.astype(jnp.float32), TOK_DEV, axis=0)
    shift_rows = jnp.repeat(shift.astype(jnp.float32), TOK_DEV, axis=0)
    scale_rows = jnp.repeat(scale.astype(jnp.float32), TOK_DEV, axis=0)
    updated = residual.astype(jnp.float32) + gate_rows * projected
    stream = updated.astype(jnp.bfloat16)
    row_mean = lax.optimization_barrier(jnp.mean(updated, axis=1, keepdims=True))
    row_var = lax.optimization_barrier(jnp.mean(jnp.square(updated - row_mean), axis=1, keepdims=True))
    normed = ((updated - row_mean) * lax.rsqrt(row_var + EPS) * (1.0 + scale_rows) + shift_rows).astype(jnp.bfloat16)
    return (stream, normed, cross_out)
```

```python
import functools
import math

import jax
import jax.numpy as jnp
from jax import lax
from jax.experimental import pallas as pl
from jax.experimental.pallas import tpu as pltpu
from jax.sharding import PartitionSpec as P

HD = 128
CAP = 2
EPS = 1e-06
VMEM_LIMIT = 48 * 1024 * 1024


def pack_kernel(peers, me_ref, dest_ref, page_ref, keys_ref, values_ref, *refs):
    out_refs, (table, count, sems) = refs[:peers], refs[peers:]

    @pl.loop(0, peers)
    def _(r):
        count[r] = 0
        for c in range(CAP):
            table[r * CAP + c] = 0

    @pl.loop(0, dest_ref.shape[0])
    def _(i):
        r = dest_ref[i]
        c = jnp.minimum(count[r], CAP - 1)
        table[r * CAP + c] = page_ref[i]
        count[r] = c + 1

    copies = []
    for k in range(peers):
        r = jnp.bitwise_xor(me_ref[0], k)
        for c in range(CAP):
            page = table[r * CAP + c]
            for half, source in enumerate((keys_ref, values_ref)):
                copy = pltpu.make_async_copy(
                    source.at[page], out_refs[k].at[half, c], sems.at[(k * CAP + c) * 2 + half]
                )
                copy.start()
                copies.append(copy)
    for copy in copies:
        copy.wait()


def pack_pages(me, dest, pages, cache_keys, cache_values, peers):
    _, page_len, width = cache_keys.shape
    smem = pl.BlockSpec(memory_space=pltpu.SMEM)
    hbm = pl.BlockSpec(memory_space=pl.ANY)
    return pl.pallas_call(
        functools.partial(pack_kernel, peers),
        out_shape=[jax.ShapeDtypeStruct((2, CAP, page_len, width), cache_keys.dtype)] * peers,
        in_specs=[smem, smem, smem, hbm, hbm],
        out_specs=[hbm] * peers,
        scratch_shapes=[
            pltpu.SMEM((peers * CAP,), jnp.int32),
            pltpu.SMEM((peers,), jnp.int32),
            pltpu.SemaphoreType.DMA((peers * CAP * 2,)),
        ],
        name="pack_pages",
    )(me, dest, pages, cache_keys, cache_values)


def resident_kernel(table_ref, keys_ref, values_ref, out_keys, out_values, sems):
    copies = []
    for j in range(table_ref.shape[0]):
        page = table_ref[j]
        for half, (source, target) in enumerate(((keys_ref, out_keys), (values_ref, out_values))):
            copy = pltpu.make_async_copy(source.at[page], target.at[j], sems.at[j * 2 + half])
            copy.start()
            copies.append(copy)
    for copy in copies:
        copy.wait()


def resident_pages(table, cache_keys, cache_values):
    pages = table.shape[0]
    hbm = pl.BlockSpec(memory_space=pl.ANY)
    shape = jax.ShapeDtypeStruct((pages,) + cache_keys.shape[1:], cache_keys.dtype)
    return pl.pallas_call(
        resident_kernel,
        out_shape=[shape, shape],
        in_specs=[pl.BlockSpec(memory_space=pltpu.SMEM), hbm, hbm],
        out_specs=[hbm, hbm],
        scratch_shapes=[pltpu.SemaphoreType.DMA((pages * 2,))],
        name="resident_pages",
    )(table, cache_keys, cache_values)


def softmax_head(query, keys, values, bias):
    factor = math.log2(math.e) / math.sqrt(HD)
    scores = lax.dot_general(
        query, keys, (((1,), (1,)), ((), ())), preferred_element_type=jnp.float32
    )
    if bias is not None:
        scores = scores + bias
    row_max = jnp.max(scores, axis=1, keepdims=True)
    exponent = jnp.exp2((scores - row_max) * factor)
    denominator = jnp.sum(exponent, axis=1, keepdims=True)
    mixed = jnp.dot(exponent.astype(jnp.bfloat16), values, preferred_element_type=jnp.float32)
    return (mixed / denominator).astype(jnp.bfloat16)


def self_kernel(heads, bias_ref, q_ref, rk_ref, rv_ref, k_ref, v_ref, *refs):
    arrived, out_ref = refs[:-1], refs[-1]
    for h in range(heads):
        part = slice(h * HD, (h + 1) * HD)
        keys = [rk_ref[:, :, part].reshape(-1, HD)]
        values = [rv_ref[:, :, part].reshape(-1, HD)]
        for a in arrived:
            keys.append(a[0, :, :, part].reshape(-1, HD))
            values.append(a[1, :, :, part].reshape(-1, HD))
        keys.append(k_ref[:, part])
        values.append(v_ref[:, part])
        out_ref[:, part] = softmax_head(
            q_ref[:, part], jnp.concatenate(keys, axis=0), jnp.concatenate(values, axis=0), bias_ref[...]
        )


def cross_kernel(heads, q_ref, k_ref, v_ref, out_ref):
    for h in range(heads):
        part = slice(h * HD, (h + 1) * HD)
        out_ref[:, part] = softmax_head(q_ref[:, part], k_ref[:, part], v_ref[:, part], None)


def head_group(width):
    heads = width // HD
    for group in (5, 4, 2):
        if heads % group == 0:
            return group
    return 1


def self_attention(bias, query, res_keys, res_values, keys, values, arrived):
    tokens, width = query.shape
    group = head_group(width)
    block = group * HD
    flat = lambda rows: pl.BlockSpec((rows, block), lambda h: (0, h))
    paged = pl.BlockSpec(res_keys.shape[:2] + (block,), lambda h: (0, 0, h))
    moved = pl.BlockSpec(arrived[0].shape[:3] + (block,), lambda h: (0, 0, 0, h))
    count = bias.shape[1]
    return pl.pallas_call(
        functools.partial(self_kernel, group),
        out_shape=jax.ShapeDtypeStruct((tokens, width), query.dtype),
        grid=(width // block,),
        in_specs=[pl.BlockSpec(bias.shape, lambda h: (0, 0)), flat(tokens), paged, paged, flat(tokens), flat(tokens)]
        + [moved] * len(arrived),
        out_specs=flat(tokens),
        compiler_params=pltpu.CompilerParams(vmem_limit_bytes=VMEM_LIMIT),
        cost_estimate=pl.CostEstimate(
            flops=4 * tokens * count * width,
            bytes_accessed=2 * width * (2 * tokens + 2 * count),
            transcendentals=tokens * count * width // HD,
        ),
        name="self_attention",
    )(bias, query, res_keys, res_values, keys, values, *arrived)


def cross_attention(query, keys, values):
    tokens, width = query.shape
    group = head_group(width)
    block = group * HD
    flat = lambda rows: pl.BlockSpec((rows, block), lambda h: (0, h))
    count = keys.shape[0]
    return pl.pallas_call(
        functools.partial(cross_kernel, group),
        out_shape=jax.ShapeDtypeStruct((tokens, width), query.dtype),
        grid=(width // block,),
        in_specs=[flat(tokens), flat(count), flat(count)],
        out_specs=flat(tokens),
        compiler_params=pltpu.CompilerParams(vmem_limit_bytes=VMEM_LIMIT),
        cost_estimate=pl.CostEstimate(
            flops=4 * tokens * count * width,
            bytes_accessed=2 * width * (2 * tokens + 2 * count),
            transcendentals=tokens * count * width // HD,
        ),
        name="cross_attention",
    )(query, keys, values)


def tp_sum(x):
    if lax.axis_size("tp") == 2:
        return x + lax.ppermute(x, "tp", [(0, 1), (1, 0)])
    return lax.psum(x, "tp")


def after(x, *earlier):
    return lax.optimization_barrier((x,) + earlier)[0]


def swap(x, bits):
    size = lax.axis_size("req")
    return lax.ppermute(x, "req", [(i, i ^ bits) for i in range(size)])


def partial_product(rows, weights):
    return jnp.dot(rows, weights, preferred_element_type=jnp.float32)


def projection_gathered(attended, out_weight):
    width = attended.shape[1]
    weights = lax.all_gather(out_weight, "req", axis=1, tiled=True)
    partial = partial_product(attended, weights).astype(jnp.bfloat16)
    column = lax.axis_index("tp") * width
    if lax.axis_size("tp") == 2:
        other = (lax.axis_size("tp") - 1) * width - column
        own = lax.dynamic_slice_in_dim(partial, column, width, 1)
        sent = lax.dynamic_slice_in_dim(partial, other, width, 1)
        received = lax.ppermute(sent, "tp", [(0, 1), (1, 0)])
        return own.astype(jnp.float32) + received.astype(jnp.float32)
    summed = lax.psum(partial, "tp").astype(jnp.float32)
    return lax.dynamic_slice_in_dim(summed, column, width, 1)


CORE, Y, Z1, Z2 = 1, 2, 4, 8
CHUNKS = 5


def projection_planes(attended, out_weight, pages_in):
    tokens, width = attended.shape
    shard = out_weight.shape[1]
    me, x = lax.axis_index("req"), lax.axis_index("tp")
    core, z_low, z_high = me % 2, (me // 4) % 2, me // 8
    half = width // 2

    mine = lax.dynamic_slice_in_dim(out_weight, core * half, half, 0)
    other = lax.dynamic_slice_in_dim(out_weight, (1 - core) * half, half, 0)
    got = swap(other, CORE)
    block = jnp.where(
        core == 0, jnp.concatenate([mine, got], axis=1), jnp.concatenate([got, mine], axis=1)
    )
    block_y = swap(block, Y)

    early_mine = jnp.concatenate([block, block_y], axis=1)
    early_other = swap(early_mine, CORE)

    step = 2 * shard // CHUNKS
    late = []
    gate_on = list(pages_in)
    for j in range(CHUNKS):
        piece = lax.slice_in_dim(block, j * step, (j + 1) * step, axis=1)
        piece = swap(after(piece, *gate_on), Z2)
        late_mine = jnp.concatenate([piece, swap(piece, Y)], axis=1)
        late.append((late_mine, swap(late_mine, CORE)))
        gate_on = [late[-2][0]] if j >= 1 else gate_on

    both = jnp.concatenate([attended, swap(attended, Z1)], axis=0)
    rows_mine = lax.dynamic_slice_in_dim(both, core * half, half, 1)
    rows_other = lax.dynamic_slice_in_dim(both, (1 - core) * half, half, 1)

    def product(w_mine, w_other):
        return (partial_product(rows_mine, w_mine) + partial_product(rows_other, w_other)).astype(jnp.bfloat16)

    ids = [(r, t) for r in range(16) for t in range(2)]
    flat = lambda r, t: r * 2 + t

    def deliver(partial, late_half):
        owners = [(r, t) for r, t in ids if t == ((r // 8) ^ late_half)]
        others = [(r, t) for r, t in ids if t != ((r // 8) ^ late_half)]
        axes = ("req", "tp")
        own, neighbour = partial[:tokens], partial[tokens:]
        from_x = lax.ppermute(own, axes, [(flat(r, t), flat(r, 1 - t)) for r, t in others])
        from_z = lax.ppermute(neighbour, axes, [(flat(r, t), flat(r ^ Z1, t)) for r, t in owners])
        from_xz = lax.ppermute(neighbour, axes, [(flat(r, t), flat(r ^ Z1, 1 - t)) for r, t in others])
        own_sum = own.astype(jnp.float32) + from_x.astype(jnp.float32)
        other_sum = from_z.astype(jnp.float32) + from_xz.astype(jnp.float32)
        return own_sum, other_sum

    early_own, early_neigh = deliver(product(early_mine, early_other), 0)
    late_parts = [deliver(product(a, b), 1) for a, b in late]
    block_width = 2 * shard

    def late_columns(i):
        first = [p[i][:, :step] for p in late_parts]
        second = [p[i][:, step:] for p in late_parts]
        return jnp.concatenate(first + second, axis=1)

    def ordered(a):
        y = (me // 2) % 2
        a0, a1 = a[:, :block_width], a[:, block_width:]
        return jnp.where(y == 0, jnp.concatenate([a0, a1], axis=1), jnp.concatenate([a1, a0], axis=1))

    is_early = x == z_high
    own_cols = ordered(jnp.where(is_early, early_own, late_columns(0)))
    neigh_cols = ordered(jnp.where(is_early, early_neigh, late_columns(1)))
    return jnp.where(
        z_low == 0,
        jnp.concatenate([own_cols, neigh_cols], axis=1),
        jnp.concatenate([neigh_cols, own_cols], axis=1),
    )


def shards(
    queries,
    new_keys,
    new_values,
    query_gain,
    key_gain,
    cache_keys,
    cache_values,
    page_table,
    cache_lens,
    mig_pages,
    mig_dest,
    cross_queries,
    text_keys,
    text_values,
    out_weight,
    residual,
    gate,
    shift,
    scale,
):
    tokens, width = queries.shape
    tp, peers = lax.axis_size("tp"), lax.axis_size("req")
    full_width = width * tp
    me = lax.axis_index("req")
    page_len = cache_keys.shape[1]

    packed = pack_pages(
        me.reshape(1).astype(jnp.int32), mig_dest[:, 0], mig_pages[0], cache_keys, cache_values, peers
    )
    arrived = [packed[0]] + [swap(packed[k], k) for k in range(1, peers)]
    all_dest = lax.all_gather(mig_dest[:, 0], "req", axis=0)
    filled = jnp.sum((all_dest == me).astype(jnp.int32), axis=1)
    filled = filled[jnp.bitwise_xor(jnp.arange(peers, dtype=jnp.int32), me)]
    slots = jnp.arange(CAP * page_len, dtype=jnp.int32) // page_len
    arrived_usable = (slots[None, :] < filled[:, None]).reshape(-1)

    query_float = queries.astype(jnp.float32)
    key_float = new_keys.astype(jnp.float32)
    squares = tp_sum(
        jnp.stack([jnp.sum(query_float * query_float, axis=1), jnp.sum(key_float * key_float, axis=1)])
    )
    inverse = lax.rsqrt(squares / full_width + EPS)
    query_normed = (query_float * inverse[0][:, None] * query_gain).astype(jnp.bfloat16)
    key_normed = (key_float * inverse[1][:, None] * key_gain).astype(jnp.bfloat16)

    res_keys, res_values = resident_pages(page_table[0], cache_keys, cache_values)
    resident_usable = jnp.arange(res_keys.shape[0] * page_len, dtype=jnp.int32) < cache_lens[0]
    usable = jnp.concatenate([resident_usable, arrived_usable, jnp.ones((tokens,), bool)])
    bias = jnp.where(usable, 0.0, -jnp.inf).astype(jnp.float32)[None, :]

    cross_out = cross_attention(cross_queries, text_keys, text_values)
    attended = self_attention(bias, query_normed, res_keys, res_values, key_normed, new_values, arrived)

    if peers == 16 and tp == 2:
        projected = projection_planes(attended, out_weight, arrived)
    else:
        projected = projection_gathered(attended, out_weight)

    updated = residual.astype(jnp.float32) + gate.astype(jnp.float32) * projected
    stream = updated.astype(jnp.bfloat16)
    local_mean = jnp.mean(updated, axis=1)
    local_square = jnp.sum(jnp.square(updated - local_mean[:, None]), axis=1)
    if tp == 2:
        theirs = lax.ppermute(jnp.stack([local_mean, local_square]), "tp", [(0, 1), (1, 0)])
        row_mean = (local_mean + theirs[0]) * 0.5
        gap = local_mean - theirs[0]
        row_var = (local_square + theirs[1] + gap * gap * (0.5 * width)) / full_width
    else:
        row_mean = lax.psum(local_mean, "tp") / tp
        offset = local_mean - row_mean
        row_var = lax.psum(local_square + width * offset * offset, "tp") / full_width
    normed = (
        (updated - row_mean[:, None]) * lax.rsqrt(row_var + EPS)[:, None] * (1.0 + scale.astype(jnp.float32))
        + shift.astype(jnp.float32)
    ).astype(jnp.bfloat16)
    return (stream, normed, cross_out)


def solution(mesh):
    in_specs = (
        P("req", "tp"),
        P("req", "tp"),
        P("req", "tp"),
        P("tp"),
        P("tp"),
        P("req", None, "tp"),
        P("req", None, "tp"),
        P("req", None),
        P("req"),
        P("req", None),
        P("req", None),
        P("req", "tp"),
        P("req", "tp"),
        P("req", "tp"),
        P("tp", "req"),
        P("req", "tp"),
        P("req", "tp"),
        P("req", "tp"),
        P("req", "tp"),
    )
    out_specs = (P("req", "tp"), P("req", "tp"), P("req", "tp"))
    return jax.shard_map(shards, mesh=mesh, in_specs=in_specs, out_specs=out_specs, check_vma=False)
```

```python
import functools
import math

import jax
import jax.numpy as jnp
from jax import lax
from jax.experimental import pallas as pl
from jax.experimental.pallas import tpu as pltpu
from jax.sharding import PartitionSpec as P

HD = 128
CAP = 2
EPS = 1e-06
VMEM_LIMIT = 48 * 1024 * 1024
COST = pl.CostEstimate(flops=1, bytes_accessed=1, transcendentals=0)


def pack_kernel(dest_ref, page_ref, keys_ref, values_ref, out_ref, table, count, sems):
    peers = count.shape[0]

    @pl.loop(0, peers)
    def _(r):
        count[r] = 0

    @pl.loop(0, dest_ref.shape[0])
    def _(i):
        r = dest_ref[i, 0]
        c = jnp.minimum(count[r], CAP - 1)
        table[r * CAP + c] = page_ref[0, i]
        count[r] = c + 1

    def copies(slot, page):
        return [
            pltpu.make_async_copy(source.at[page], out_ref.at[slot, half], sems.at[slot * 2 + half])
            for half, source in enumerate((keys_ref, values_ref))
        ]

    for r in range(peers):
        for c in range(CAP):
            slot = r * CAP + c

            @pl.when(c < count[r])
            def _():
                for copy in copies(slot, table[slot]):
                    copy.start()

            @pl.when(c >= count[r])
            def _():
                out_ref[slot, 0] = jnp.full(out_ref.shape[2:], jnp.inf, out_ref.dtype)
                out_ref[slot, 1] = jnp.zeros(out_ref.shape[2:], out_ref.dtype)

    for r in range(peers):
        for c in range(CAP):
            slot = r * CAP + c

            @pl.when(c < count[r])
            def _():
                for copy in copies(slot, 0):
                    copy.wait()


def pack_pages(dest, pages, cache_keys, cache_values, peers):
    _, page_len, width = cache_keys.shape
    smem = pl.BlockSpec(memory_space=pltpu.SMEM)
    hbm = pl.BlockSpec(memory_space=pl.ANY)
    return pl.pallas_call(
        pack_kernel,
        out_shape=jax.ShapeDtypeStruct((peers * CAP, 2, page_len, width), cache_keys.dtype),
        in_specs=[smem, smem, hbm, hbm],
        out_specs=pl.BlockSpec(memory_space=pltpu.VMEM),
        scratch_shapes=[
            pltpu.SMEM((peers * CAP,), jnp.int32),
            pltpu.SMEM((peers,), jnp.int32),
            pltpu.SemaphoreType.DMA((peers * CAP * 2,)),
        ],
        compiler_params=pltpu.CompilerParams(vmem_limit_bytes=VMEM_LIMIT),
        cost_estimate=COST,
        name="pack_pages",
    )(dest, pages, cache_keys, cache_values)


def resident_kernel(table_ref, keys_ref, values_ref, out_keys, out_values, sems):
    copies = []
    for j in range(table_ref.shape[0]):
        page = table_ref[j]
        for half, (source, target) in enumerate(((keys_ref, out_keys), (values_ref, out_values))):
            copy = pltpu.make_async_copy(source.at[page], target.at[j], sems.at[j * 2 + half])
            copy.start()
            copies.append(copy)
    for copy in copies:
        copy.wait()


def resident_pages(table, cache_keys, cache_values):
    pages = table.shape[0]
    hbm = pl.BlockSpec(memory_space=pl.ANY)
    vmem = pl.BlockSpec(memory_space=pltpu.VMEM)
    shape = jax.ShapeDtypeStruct((pages,) + cache_keys.shape[1:], cache_keys.dtype)
    return pl.pallas_call(
        resident_kernel,
        out_shape=[shape, shape],
        in_specs=[pl.BlockSpec(memory_space=pltpu.SMEM), hbm, hbm],
        out_specs=[vmem, vmem],
        scratch_shapes=[pltpu.SemaphoreType.DMA((pages * 2,))],
        compiler_params=pltpu.CompilerParams(vmem_limit_bytes=VMEM_LIMIT),
        cost_estimate=COST,
        name="resident_pages",
    )(table, cache_keys, cache_values)


STAT_ROWS = 16
FACTOR = math.log2(math.e) / math.sqrt(HD)


def head_scores(query, keys):
    return lax.dot_general(keys, query, (((1,), (1,)), ((), ())), preferred_element_type=jnp.float32)


def weigh(scores, row_max, values):
    exponent = jnp.exp2((scores - row_max) * FACTOR)
    mixed = lax.dot_general(
        values, exponent.astype(jnp.bfloat16), (((0,), (0,)), ((), ())), preferred_element_type=jnp.float32
    )
    return mixed, jnp.sum(exponent, axis=0, keepdims=True)


def local_kernel(heads, length_ref, q_ref, rk_ref, rv_ref, k_ref, v_ref, sum_ref, stat_ref):
    resident = rk_ref.shape[0] * rk_ref.shape[1]
    position = lax.broadcasted_iota(jnp.int32, (resident, q_ref.shape[0]), 0)
    for h in range(heads):
        part = slice(h * HD, (h + 1) * HD)
        query = q_ref[:, part]
        values = jnp.concatenate([rv_ref[:, :, part].reshape(-1, HD), v_ref[:, part]], axis=0)
        paged = head_scores(query, rk_ref[:, :, part].reshape(-1, HD))
        paged = jnp.where(position < length_ref[0], paged, -jnp.inf)
        scores = jnp.concatenate([paged, head_scores(query, k_ref[:, part])], axis=0)
        row_max = jnp.max(scores, axis=0, keepdims=True)
        mixed, denominator = weigh(scores, row_max, values)
        sum_ref[part] = mixed
        stat_ref[0, 2 * h : 2 * h + 1] = row_max
        stat_ref[0, 2 * h + 1 : 2 * h + 2] = denominator


def arrived_kernel(heads, usable_ref, q_ref, arrived_ref, sum_ref, stat_ref, out_ref):
    for h in range(heads):
        part = slice(h * HD, (h + 1) * HD)
        scores = head_scores(q_ref[:, part], arrived_ref[:, 0, :, part].reshape(-1, HD))
        scores = jnp.where(usable_ref[...] > 0, scores, -jnp.inf)
        local_max = stat_ref[0, 2 * h : 2 * h + 1]
        row_max = jnp.maximum(local_max, jnp.max(scores, axis=0, keepdims=True))
        mixed, denominator = weigh(scores, row_max, arrived_ref[:, 1, :, part].reshape(-1, HD))
        carry = jnp.exp2((local_max - row_max) * FACTOR)
        denominator = denominator + stat_ref[0, 2 * h + 1 : 2 * h + 2] * carry
        mixed = (mixed + sum_ref[part] * carry) / denominator
        out_ref[:, part] = jnp.transpose(mixed).astype(jnp.bfloat16)


def cross_kernel(heads, q_ref, k_ref, v_ref, out_ref):
    for h in range(heads):
        part = slice(h * HD, (h + 1) * HD)
        scores = head_scores(q_ref[:, part], k_ref[:, part])
        mixed, denominator = weigh(scores, jnp.max(scores, axis=0, keepdims=True), v_ref[:, part])
        out_ref[:, part] = jnp.transpose(mixed / denominator).astype(jnp.bfloat16)


def head_group(heads):
    for group in (5, 4, 3, 2):
        if heads % group == 0:
            return group
    return 1


def local_attention(length, query, res_keys, res_values, keys, values):
    tokens, width = query.shape
    group = head_group(width // HD)
    block = group * HD
    steps = width // block
    flat = pl.BlockSpec((tokens, block), lambda h: (0, h))
    paged = pl.BlockSpec(res_keys.shape[:2] + (block,), lambda h: (0, 0, h))
    return pl.pallas_call(
        functools.partial(local_kernel, group),
        out_shape=[
            jax.ShapeDtypeStruct((width, tokens), jnp.float32),
            jax.ShapeDtypeStruct((steps, STAT_ROWS, tokens), jnp.float32),
        ],
        grid=(steps,),
        in_specs=[pl.BlockSpec(memory_space=pltpu.SMEM), flat, paged, paged, flat, flat],
        out_specs=[
            pl.BlockSpec((block, tokens), lambda h: (h, 0)),
            pl.BlockSpec((1, STAT_ROWS, tokens), lambda h: (h, 0, 0)),
        ],
        compiler_params=pltpu.CompilerParams(vmem_limit_bytes=VMEM_LIMIT),
        cost_estimate=COST,
        name="local_attention",
    )(length, query, res_keys, res_values, keys, values)


def arrived_attention(usable, query, arrived, sums, stats):
    tokens, width = query.shape
    steps = stats.shape[0]
    block = width // steps
    flat = pl.BlockSpec((tokens, block), lambda h: (0, h))
    return pl.pallas_call(
        functools.partial(arrived_kernel, block // HD),
        out_shape=jax.ShapeDtypeStruct((tokens, width), query.dtype),
        grid=(steps,),
        in_specs=[
            pl.BlockSpec(usable.shape, lambda h: (0, 0)),
            flat,
            pl.BlockSpec(arrived.shape[:3] + (block,), lambda h: (0, 0, 0, h)),
            pl.BlockSpec((block, tokens), lambda h: (h, 0)),
            pl.BlockSpec((1, STAT_ROWS, tokens), lambda h: (h, 0, 0)),
        ],
        out_specs=flat,
        compiler_params=pltpu.CompilerParams(vmem_limit_bytes=VMEM_LIMIT),
        cost_estimate=COST,
        name="arrived_attention",
    )(usable, query, arrived, sums, stats)


def cross_attention(query, keys, values):
    tokens, width = query.shape
    group = head_group(width // HD)
    block = group * HD
    flat = lambda rows: pl.BlockSpec((rows, block), lambda h: (0, h))
    count = keys.shape[0]
    return pl.pallas_call(
        functools.partial(cross_kernel, group),
        out_shape=jax.ShapeDtypeStruct((tokens, width), query.dtype),
        grid=(width // block,),
        in_specs=[flat(tokens), flat(count), flat(count)],
        out_specs=flat(tokens),
        compiler_params=pltpu.CompilerParams(vmem_limit_bytes=VMEM_LIMIT),
        cost_estimate=COST,
        name="cross_attention",
    )(query, keys, values)


def tp_sum(x):
    if lax.axis_size("tp") == 2:
        return x + lax.ppermute(x, "tp", [(0, 1), (1, 0)])
    return lax.psum(x, "tp")


def after(x, *earlier):
    return lax.optimization_barrier((x,) + earlier)[0]


def swap(x, bits):
    size = lax.axis_size("req")
    return lax.ppermute(x, "req", [(i, i ^ bits) for i in range(size)])


def partial_product(rows, weights):
    return jnp.dot(rows, weights, preferred_element_type=jnp.float32)


def projection_gathered(attended, out_weight):
    width = attended.shape[1]
    weights = lax.all_gather(out_weight, "req", axis=1, tiled=True)
    partial = partial_product(attended, weights).astype(jnp.bfloat16)
    column = lax.axis_index("tp") * width
    if lax.axis_size("tp") == 2:
        other = (lax.axis_size("tp") - 1) * width - column
        own = lax.dynamic_slice_in_dim(partial, column, width, 1)
        sent = lax.dynamic_slice_in_dim(partial, other, width, 1)
        received = lax.ppermute(sent, "tp", [(0, 1), (1, 0)])
        return own.astype(jnp.float32) + received.astype(jnp.float32)
    summed = lax.psum(partial, "tp").astype(jnp.float32)
    return lax.dynamic_slice_in_dim(summed, column, width, 1)


CORE, Y, Z1, Z2 = 1, 2, 4, 8
PIECES = (2, 2, 1)


def planes_weights(out_weight):
    half = out_weight.shape[0] // 2
    core = lax.axis_index("req") % 2
    mine = lax.dynamic_slice_in_dim(out_weight, core * half, half, 0)
    other = lax.dynamic_slice_in_dim(out_weight, (1 - core) * half, half, 0)
    got = swap(other, CORE)
    block = jnp.where(core == 0, jnp.concatenate([mine, got], axis=1), jnp.concatenate([got, mine], axis=1))
    unit = block.shape[1] // sum(PIECES)
    ends = [sum(PIECES[: j + 1]) * unit for j in range(len(PIECES))]
    return block, [lax.slice_in_dim(block, e - p * unit, e, axis=1) for e, p in zip(ends, PIECES)]


def planes_projection(block, pieces, late_0, arrived, attended):
    half = block.shape[0]
    tokens = attended.shape[0]
    me, x = lax.axis_index("req"), lax.axis_index("tp")
    core, y, z_low, z_high = me % 2, (me // 2) % 2, (me // 4) % 2, me // 8
    own_early = x == z_high

    block_y = after(swap(block, Y), attended)
    late = after(late_0, attended)
    rows = jnp.concatenate([attended, swap(attended, Z1)], axis=0)
    rows_mine = jnp.where(core == 0, rows[:, :half], rows[:, half:])
    rows_other = jnp.where(core == 0, rows[:, half:], rows[:, :half])

    def product(w):
        w_other = swap(w, CORE)
        return (partial_product(rows_mine, w) + partial_product(rows_other, w_other)).astype(jnp.bfloat16)

    early = product(block), product(block_y)
    own_parts, near_parts = [], []
    first = 0
    for j, piece in enumerate(pieces):
        size = piece.shape[1]
        if j == 1:
            arrival = swap(after(piece, late_0, attended), Z2)
            late = after(arrival, rows_mine)
        if j > 1:
            arrival = swap(after(piece, arrival), Z2)
            arrival = late = after(arrival, first_sent)
        late_part = product(jnp.concatenate([late, swap(late, Y)], axis=1))
        early_part = jnp.concatenate([e[:, first : first + size] for e in early], axis=1)
        first += size
        kept = jnp.where(own_early, early_part, late_part)
        sent = jnp.where(own_early, late_part, early_part)
        if j == 0:
            first_sent = sent
        received = lax.ppermute(sent, "tp", [(0, 1), (1, 0)])
        total = kept.astype(jnp.float32) + received.astype(jnp.float32)
        own_parts.append(total[:tokens])
        near_parts.append(swap(total[tokens:].astype(jnp.bfloat16), Z1).astype(jnp.float32))

    def ordered(parts):
        this = jnp.concatenate([p[:, : p.shape[1] // 2] for p in parts], axis=1)
        that = jnp.concatenate([p[:, p.shape[1] // 2 :] for p in parts], axis=1)
        return jnp.where(y == 0, jnp.concatenate([this, that], axis=1), jnp.concatenate([that, this], axis=1))

    own, near = ordered(own_parts), ordered(near_parts)
    return jnp.where(z_low == 0, jnp.concatenate([own, near], axis=1), jnp.concatenate([near, own], axis=1))


def shards(
    queries,
    new_keys,
    new_values,
    query_gain,
    key_gain,
    cache_keys,
    cache_values,
    page_table,
    cache_lens,
    mig_pages,
    mig_dest,
    cross_queries,
    text_keys,
    text_values,
    out_weight,
    residual,
    gate,
    shift,
    scale,
):
    tokens, width = queries.shape
    tp, peers = lax.axis_size("tp"), lax.axis_size("req")
    full_width = width * tp
    me = lax.axis_index("req")
    page_len = cache_keys.shape[1]

    packed = pack_pages(mig_dest, mig_pages, cache_keys, cache_values, peers)
    arrived = lax.all_to_all(packed, "req", split_axis=0, concat_axis=0, tiled=True)
    filled = (arrived[:, 0, 0, 0] < jnp.inf).astype(jnp.float32)
    arrived_usable = jnp.broadcast_to(filled[:, None, None], (filled.shape[0], page_len, tokens)).reshape(-1, tokens)

    planes = peers == 16 and tp == 2
    if planes:
        block, pieces = planes_weights(out_weight)
        page_table, cross_queries = after(page_table, block, *pieces), after(cross_queries, block, *pieces)

    query_float = queries.astype(jnp.float32)
    key_float = new_keys.astype(jnp.float32)
    squares = tp_sum(
        jnp.stack([jnp.sum(query_float * query_float, axis=1), jnp.sum(key_float * key_float, axis=1)])
    )
    inverse = lax.rsqrt(squares / full_width + EPS)
    query_normed = (query_float * inverse[0][:, None] * query_gain).astype(jnp.bfloat16)
    key_normed = (key_float * inverse[1][:, None] * key_gain).astype(jnp.bfloat16)

    res_keys, res_values = resident_pages(page_table[0], cache_keys, cache_values)
    sums, stats = local_attention(cache_lens, query_normed, res_keys, res_values, key_normed, new_values)
    cross_out = cross_attention(cross_queries, text_keys, text_values)
    sums = after(sums, cross_out)
    if planes:
        late_0 = swap(after(pieces[0], sums), Z2)
    attended = arrived_attention(arrived_usable, query_normed, arrived, sums, stats)
    if planes:
        projected = planes_projection(block, pieces, late_0, arrived, attended)
    else:
        projected = projection_gathered(attended, out_weight)

    updated = residual.astype(jnp.float32) + gate.astype(jnp.float32) * projected
    stream = updated.astype(jnp.bfloat16)
    local_mean = jnp.mean(updated, axis=1)
    local_square = jnp.sum(jnp.square(updated - local_mean[:, None]), axis=1)
    if tp == 2:
        theirs = lax.ppermute(jnp.stack([local_mean, local_square]), "tp", [(0, 1), (1, 0)])
        row_mean = (local_mean + theirs[0]) * 0.5
        gap = local_mean - theirs[0]
        row_var = (local_square + theirs[1] + gap * gap * (0.5 * width)) / full_width
    else:
        row_mean = lax.psum(local_mean, "tp") / tp
        offset = local_mean - row_mean
        row_var = lax.psum(local_square + width * offset * offset, "tp") / full_width
    normed = (
        (updated - row_mean[:, None]) * lax.rsqrt(row_var + EPS)[:, None] * (1.0 + scale.astype(jnp.float32))
        + shift.astype(jnp.float32)
    ).astype(jnp.bfloat16)
    return (stream, normed, cross_out)


def solution(mesh):
    in_specs = (
        P("req", "tp"),
        P("req", "tp"),
        P("req", "tp"),
        P("tp"),
        P("tp"),
        P("req", None, "tp"),
        P("req", None, "tp"),
        P("req", None),
        P("req"),
        P("req", None),
        P("req", None),
        P("req", "tp"),
        P("req", "tp"),
        P("req", "tp"),
        P("tp", "req"),
        P("req", "tp"),
        P("req", "tp"),
        P("req", "tp"),
        P("req", "tp"),
    )
    out_specs = (P("req", "tp"), P("req", "tp"), P("req", "tp"))
    return jax.shard_map(shards, mesh=mesh, in_specs=in_specs, out_specs=out_specs, check_vma=False)
```

```python
import functools
import math

import jax
import jax.numpy as jnp
from jax import lax
from jax.experimental import pallas as pl
from jax.experimental.pallas import tpu as pltpu
from jax.sharding import PartitionSpec as P

HD = 128
CAP = 2
EPS = 1e-06
VMEM_LIMIT = 48 * 1024 * 1024
PACK_LIMIT = 60 * 1024 * 1024
COST = pl.CostEstimate(flops=1, bytes_accessed=1, transcendentals=0)


def pack_kernel(dest_ref, page_ref, keys_ref, values_ref, out_ref, table, count, sems):
    peers = count.shape[0]

    @pl.loop(0, peers)
    def _(r):
        count[r] = 0

    @pl.loop(0, dest_ref.shape[0])
    def _(i):
        r = dest_ref[i, 0]
        c = jnp.minimum(count[r], CAP - 1)
        table[r * CAP + c] = page_ref[0, i]
        count[r] = c + 1

    def copies(slot, page):
        return [
            pltpu.make_async_copy(source.at[page], out_ref.at[slot, half], sems.at[slot * 2 + half])
            for half, source in enumerate((keys_ref, values_ref))
        ]

    for r in range(peers):
        for c in range(CAP):
            slot = r * CAP + c

            @pl.when(c < count[r])
            def _():
                for copy in copies(slot, table[slot]):
                    copy.start()

            @pl.when(c >= count[r])
            def _():
                out_ref[slot, 0] = jnp.full(out_ref.shape[2:], jnp.inf, out_ref.dtype)
                out_ref[slot, 1] = jnp.zeros(out_ref.shape[2:], out_ref.dtype)

    for r in range(peers):
        for c in range(CAP):
            slot = r * CAP + c

            @pl.when(c < count[r])
            def _():
                for copy in copies(slot, 0):
                    copy.wait()


def pack_pages(dest, pages, cache_keys, cache_values, peers):
    _, page_len, width = cache_keys.shape
    smem = pl.BlockSpec(memory_space=pltpu.SMEM)
    hbm = pl.BlockSpec(memory_space=pltpu.HBM)
    return pl.pallas_call(
        pack_kernel,
        out_shape=jax.ShapeDtypeStruct((peers * CAP, 2, page_len, width), cache_keys.dtype),
        in_specs=[smem, smem, hbm, hbm],
        out_specs=pl.BlockSpec(memory_space=pltpu.VMEM),
        scratch_shapes=[
            pltpu.SMEM((peers * CAP,), jnp.int32),
            pltpu.SMEM((peers,), jnp.int32),
            pltpu.SemaphoreType.DMA((peers * CAP * 2,)),
        ],
        compiler_params=pltpu.CompilerParams(vmem_limit_bytes=PACK_LIMIT),
        cost_estimate=COST,
        name="pack_pages",
    )(dest, pages, cache_keys, cache_values)


def resident_kernel(table_ref, keys_ref, values_ref, out_keys, out_values, sems):
    copies = []
    for j in range(table_ref.shape[0]):
        page = table_ref[j]
        for half, (source, target) in enumerate(((keys_ref, out_keys), (values_ref, out_values))):
            copy = pltpu.make_async_copy(source.at[page], target.at[j], sems.at[j * 2 + half])
            copy.start()
            copies.append(copy)
    for copy in copies:
        copy.wait()


def resident_pages(table, cache_keys, cache_values):
    pages = table.shape[0]
    hbm = pl.BlockSpec(memory_space=pltpu.HBM)
    vmem = pl.BlockSpec(memory_space=pltpu.VMEM)
    shape = jax.ShapeDtypeStruct((pages,) + cache_keys.shape[1:], cache_keys.dtype)
    return pl.pallas_call(
        resident_kernel,
        out_shape=[shape, shape],
        in_specs=[pl.BlockSpec(memory_space=pltpu.SMEM), hbm, hbm],
        out_specs=[vmem, vmem],
        scratch_shapes=[pltpu.SemaphoreType.DMA((pages * 2,))],
        compiler_params=pltpu.CompilerParams(vmem_limit_bytes=PACK_LIMIT),
        cost_estimate=COST,
        name="resident_pages",
    )(table, cache_keys, cache_values)


STAT_ROWS = 16
FACTOR = math.log2(math.e) / math.sqrt(HD)


def head_scores(query, keys):
    return lax.dot_general(keys, query, (((1,), (1,)), ((), ())), preferred_element_type=jnp.float32)


def weigh(scores, row_max, values):
    exponent = jnp.exp2((scores - row_max) * FACTOR)
    mixed = lax.dot_general(
        values, exponent.astype(jnp.bfloat16), (((0,), (0,)), ((), ())), preferred_element_type=jnp.float32
    )
    return mixed, jnp.sum(exponent, axis=0, keepdims=True)


def local_kernel(heads, length_ref, q_ref, rk_ref, rv_ref, k_ref, v_ref, sum_ref, stat_ref):
    resident = rk_ref.shape[0] * rk_ref.shape[1]
    position = lax.broadcasted_iota(jnp.int32, (resident, q_ref.shape[0]), 0)
    for h in range(heads):
        part = slice(h * HD, (h + 1) * HD)
        query = q_ref[:, part]
        values = jnp.concatenate([rv_ref[:, :, part].reshape(-1, HD), v_ref[:, part]], axis=0)
        paged = head_scores(query, rk_ref[:, :, part].reshape(-1, HD))
        paged = jnp.where(position < length_ref[0], paged, -jnp.inf)
        scores = jnp.concatenate([paged, head_scores(query, k_ref[:, part])], axis=0)
        row_max = jnp.max(scores, axis=0, keepdims=True)
        mixed, denominator = weigh(scores, row_max, values)
        sum_ref[part] = mixed
        stat_ref[0, 2 * h : 2 * h + 1] = row_max
        stat_ref[0, 2 * h + 1 : 2 * h + 2] = denominator


def arrived_kernel(heads, usable_ref, q_ref, arrived_ref, sum_ref, stat_ref, out_ref):
    parts = [slice(h * HD, (h + 1) * HD) for h in range(heads)]
    usable = usable_ref[...] > 0
    scores = [head_scores(q_ref[:, part], arrived_ref[:, 0, :, part].reshape(-1, HD)) for part in parts]
    scores = [jnp.where(usable, s, -jnp.inf) for s in scores]
    local_max = [stat_ref[0, 2 * h : 2 * h + 1] for h in range(heads)]
    row_max = [jnp.maximum(m, jnp.max(s, axis=0, keepdims=True)) for m, s in zip(local_max, scores)]
    carry = [jnp.exp2((m - r) * FACTOR) for m, r in zip(local_max, row_max)]
    weighed = [
        weigh(s, r, arrived_ref[:, 1, :, part].reshape(-1, HD)) for s, r, part in zip(scores, row_max, parts)
    ]
    for h, part in enumerate(parts):
        mixed, denominator = weighed[h]
        denominator = denominator + stat_ref[0, 2 * h + 1 : 2 * h + 2] * carry[h]
        mixed = (mixed + sum_ref[part] * carry[h]) / denominator
        out_ref[:, part] = jnp.transpose(mixed).astype(jnp.bfloat16)


def cross_kernel(heads, q_ref, k_ref, v_ref, out_ref):
    for h in range(heads):
        part = slice(h * HD, (h + 1) * HD)
        scores = head_scores(q_ref[:, part], k_ref[:, part])
        mixed, denominator = weigh(scores, jnp.max(scores, axis=0, keepdims=True), v_ref[:, part])
        out_ref[:, part] = jnp.transpose(mixed / denominator).astype(jnp.bfloat16)


def head_group(heads):
    for group in (5, 4, 3, 2):
        if heads % group == 0:
            return group
    return 1


def local_attention(length, query, res_keys, res_values, keys, values):
    tokens, width = query.shape
    group = head_group(width // HD)
    block = group * HD
    steps = width // block
    flat = pl.BlockSpec((tokens, block), lambda h: (0, h))
    paged = pl.BlockSpec(res_keys.shape[:2] + (block,), lambda h: (0, 0, h))
    return pl.pallas_call(
        functools.partial(local_kernel, group),
        out_shape=[
            jax.ShapeDtypeStruct((width, tokens), jnp.float32),
            jax.ShapeDtypeStruct((steps, STAT_ROWS, tokens), jnp.float32),
        ],
        grid=(steps,),
        in_specs=[pl.BlockSpec(memory_space=pltpu.SMEM), flat, paged, paged, flat, flat],
        out_specs=[
            pl.BlockSpec((block, tokens), lambda h: (h, 0)),
            pl.BlockSpec((1, STAT_ROWS, tokens), lambda h: (h, 0, 0)),
        ],
        compiler_params=pltpu.CompilerParams(vmem_limit_bytes=VMEM_LIMIT),
        cost_estimate=COST,
        name="local_attention",
    )(length, query, res_keys, res_values, keys, values)


def arrived_attention(usable, query, arrived, sums, stats):
    tokens, width = query.shape
    steps = stats.shape[0]
    block = width // steps
    flat = pl.BlockSpec((tokens, block), lambda h: (0, h))
    return pl.pallas_call(
        functools.partial(arrived_kernel, block // HD),
        out_shape=jax.ShapeDtypeStruct((tokens, width), query.dtype),
        grid=(steps,),
        in_specs=[
            pl.BlockSpec(usable.shape, lambda h: (0, 0)),
            flat,
            pl.BlockSpec(arrived.shape[:3] + (block,), lambda h: (0, 0, 0, h)),
            pl.BlockSpec((block, tokens), lambda h: (h, 0)),
            pl.BlockSpec((1, STAT_ROWS, tokens), lambda h: (h, 0, 0)),
        ],
        out_specs=flat,
        compiler_params=pltpu.CompilerParams(vmem_limit_bytes=VMEM_LIMIT),
        cost_estimate=COST,
        name="arrived_attention",
    )(usable, query, arrived, sums, stats)


def cross_attention(query, keys, values):
    tokens, width = query.shape
    group = head_group(width // HD)
    block = group * HD
    flat = lambda rows: pl.BlockSpec((rows, block), lambda h: (0, h))
    count = keys.shape[0]
    return pl.pallas_call(
        functools.partial(cross_kernel, group),
        out_shape=jax.ShapeDtypeStruct((tokens, width), query.dtype),
        grid=(width // block,),
        in_specs=[flat(tokens), flat(count), flat(count)],
        out_specs=flat(tokens),
        compiler_params=pltpu.CompilerParams(vmem_limit_bytes=VMEM_LIMIT),
        cost_estimate=COST,
        name="cross_attention",
    )(query, keys, values)


def tp_sum(x):
    if lax.axis_size("tp") == 2:
        return x + lax.ppermute(x, "tp", [(0, 1), (1, 0)])
    return lax.psum(x, "tp")


def after(x, *earlier):
    return lax.optimization_barrier((x,) + earlier)[0]


def swap(x, bits):
    size = lax.axis_size("req")
    return lax.ppermute(x, "req", [(i, i ^ bits) for i in range(size)])


def partial_product(rows, weights):
    return jnp.dot(rows, weights, preferred_element_type=jnp.float32)


def projection_gathered(attended, out_weight):
    width = attended.shape[1]
    weights = lax.all_gather(out_weight, "req", axis=1, tiled=True)
    partial = partial_product(attended, weights).astype(jnp.bfloat16)
    column = lax.axis_index("tp") * width
    if lax.axis_size("tp") == 2:
        other = (lax.axis_size("tp") - 1) * width - column
        own = lax.dynamic_slice_in_dim(partial, column, width, 1)
        sent = lax.dynamic_slice_in_dim(partial, other, width, 1)
        received = lax.ppermute(sent, "tp", [(0, 1), (1, 0)])
        return own.astype(jnp.float32) + received.astype(jnp.float32)
    summed = lax.psum(partial, "tp").astype(jnp.float32)
    return lax.dynamic_slice_in_dim(summed, column, width, 1)


CORE, Y, Z1, Z2 = 1, 2, 4, 8
PIECES = (2, 2, 1)


def planes_weights(out_weight):
    half = out_weight.shape[0] // 2
    core = lax.axis_index("req") % 2
    mine = lax.dynamic_slice_in_dim(out_weight, core * half, half, 0)
    other = lax.dynamic_slice_in_dim(out_weight, (1 - core) * half, half, 0)
    got = swap(other, CORE)
    block = jnp.where(core == 0, jnp.concatenate([mine, got], axis=1), jnp.concatenate([got, mine], axis=1))
    unit = block.shape[1] // sum(PIECES)
    ends = [sum(PIECES[: j + 1]) * unit for j in range(len(PIECES))]
    return block, [lax.slice_in_dim(block, e - p * unit, e, axis=1) for e, p in zip(ends, PIECES)]


def planes_projection(block, block_other, pieces, late_0, arrived, attended):
    half = block.shape[0]
    tokens = attended.shape[0]
    me, x = lax.axis_index("req"), lax.axis_index("tp")
    core, y, z_low, z_high = me % 2, (me // 2) % 2, (me // 4) % 2, me // 8
    own_early = x == z_high

    block_y = after(swap(block, Y), attended)
    late = after(late_0, attended)
    rows = jnp.concatenate([attended, swap(attended, Z1)], axis=0)
    rows_mine = jnp.where(core == 0, rows[:, :half], rows[:, half:])
    rows_other = jnp.where(core == 0, rows[:, half:], rows[:, :half])

    def product(w, w_other=None):
        w_other = swap(w, CORE) if w_other is None else w_other
        return (partial_product(rows_mine, w) + partial_product(rows_other, w_other)).astype(jnp.bfloat16)

    early = product(block, block_other), product(block_y)
    own_parts, near_parts = [], []
    first = 0
    for j, piece in enumerate(pieces):
        size = piece.shape[1]
        if j == 1:
            arrival = swap(after(piece, late_0, attended), Z2)
            late = after(arrival, rows_mine)
        if j > 1:
            arrival = swap(after(piece, arrival), Z2)
            arrival = late = after(arrival, first_sent)
        late_part = product(jnp.concatenate([late, swap(late, Y)], axis=1))
        if j == 2:
            late_part = after(late_part, sent)
        early_part = jnp.concatenate([e[:, first : first + size] for e in early], axis=1)
        first += size
        kept = jnp.where(own_early, early_part, late_part)
        sent = jnp.where(own_early, late_part, early_part)
        if j == 0:
            first_sent = sent
        received = lax.ppermute(sent, "tp", [(0, 1), (1, 0)])
        total = kept.astype(jnp.float32) + received.astype(jnp.float32)
        own_parts.append(total[:tokens])
        near_parts.append(swap(total[tokens:].astype(jnp.bfloat16), Z1).astype(jnp.float32))

    def ordered(parts):
        this = jnp.concatenate([p[:, : p.shape[1] // 2] for p in parts], axis=1)
        that = jnp.concatenate([p[:, p.shape[1] // 2 :] for p in parts], axis=1)
        return jnp.where(y == 0, jnp.concatenate([this, that], axis=1), jnp.concatenate([that, this], axis=1))

    own, near = ordered(own_parts), ordered(near_parts)
    return jnp.where(z_low == 0, jnp.concatenate([own, near], axis=1), jnp.concatenate([near, own], axis=1))


def shards(
    queries,
    new_keys,
    new_values,
    query_gain,
    key_gain,
    cache_keys,
    cache_values,
    page_table,
    cache_lens,
    mig_pages,
    mig_dest,
    cross_queries,
    text_keys,
    text_values,
    out_weight,
    residual,
    gate,
    shift,
    scale,
):
    tokens, width = queries.shape
    tp, peers = lax.axis_size("tp"), lax.axis_size("req")
    full_width = width * tp
    me = lax.axis_index("req")
    page_len = cache_keys.shape[1]

    packed = pack_pages(mig_dest, mig_pages, cache_keys, cache_values, peers)
    arrived = lax.all_to_all(packed, "req", split_axis=0, concat_axis=0, tiled=True)
    filled = (arrived[:, 0, 0, 0] < jnp.inf).astype(jnp.float32)
    arrived_usable = jnp.broadcast_to(filled[:, None, None], (filled.shape[0], page_len, tokens)).reshape(-1, tokens)

    planes = peers == 16 and tp == 2
    if planes:
        block, pieces = planes_weights(out_weight)
        page_table, cross_queries = after(page_table, block, *pieces), after(cross_queries, block, *pieces)

    query_float = queries.astype(jnp.float32)
    key_float = new_keys.astype(jnp.float32)
    squares = tp_sum(
        jnp.stack([jnp.sum(query_float * query_float, axis=1), jnp.sum(key_float * key_float, axis=1)])
    )
    inverse = lax.rsqrt(squares / full_width + EPS)
    query_normed = (query_float * inverse[0][:, None] * query_gain).astype(jnp.bfloat16)
    key_normed = (key_float * inverse[1][:, None] * key_gain).astype(jnp.bfloat16)

    res_keys, res_values = resident_pages(page_table[0], cache_keys, cache_values)
    sums, stats = local_attention(cache_lens, query_normed, res_keys, res_values, key_normed, new_values)
    cross_out = cross_attention(cross_queries, text_keys, text_values)
    sums = after(sums, cross_out)
    if planes:
        block_other = swap(after(block, sums), CORE)
        late_0 = swap(after(pieces[0], block_other), Z2)
    attended = arrived_attention(arrived_usable, query_normed, arrived, sums, stats)
    if planes:
        projected = planes_projection(block, block_other, pieces, late_0, arrived, attended)
    else:
        projected = projection_gathered(attended, out_weight)

    updated = residual.astype(jnp.float32) + gate.astype(jnp.float32) * projected
    stream = updated.astype(jnp.bfloat16)
    local_mean = jnp.mean(updated, axis=1)
    local_square = jnp.sum(jnp.square(updated - local_mean[:, None]), axis=1)
    if tp == 2:
        theirs = lax.ppermute(jnp.stack([local_mean, local_square]), "tp", [(0, 1), (1, 0)])
        row_mean = (local_mean + theirs[0]) * 0.5
        gap = local_mean - theirs[0]
        row_var = (local_square + theirs[1] + gap * gap * (0.5 * width)) / full_width
    else:
        row_mean = lax.psum(local_mean, "tp") / tp
        offset = local_mean - row_mean
        row_var = lax.psum(local_square + width * offset * offset, "tp") / full_width
    normed = (
        (updated - row_mean[:, None]) * lax.rsqrt(row_var + EPS)[:, None] * (1.0 + scale.astype(jnp.float32))
        + shift.astype(jnp.float32)
    ).astype(jnp.bfloat16)
    return (stream, normed, cross_out)


def solution(mesh):
    in_specs = (
        P("req", "tp"),
        P("req", "tp"),
        P("req", "tp"),
        P("tp"),
        P("tp"),
        P("req", None, "tp"),
        P("req", None, "tp"),
        P("req", None),
        P("req"),
        P("req", None),
        P("req", None),
        P("req", "tp"),
        P("req", "tp"),
        P("req", "tp"),
        P("tp", "req"),
        P("req", "tp"),
        P("req", "tp"),
        P("req", "tp"),
        P("req", "tp"),
    )
    out_specs = (P("req", "tp"), P("req", "tp"), P("req", "tp"))
    return jax.shard_map(shards, mesh=mesh, in_specs=in_specs, out_specs=out_specs, check_vma=False)
```

```python
import functools
import math

import jax
import jax.numpy as jnp
from jax import lax
from jax.experimental import pallas as pl
from jax.experimental.pallas import tpu as pltpu
from jax.sharding import PartitionSpec as P

HD = 128
CAP = 2
EPS = 1e-06
VMEM_LIMIT = 48 * 1024 * 1024
PACK_LIMIT = 60 * 1024 * 1024
COST = pl.CostEstimate(flops=1, bytes_accessed=1, transcendentals=0)


def pack_kernel(dest_ref, page_ref, keys_ref, values_ref, out_ref, table, count, sems):
    peers = count.shape[0]

    @pl.loop(0, peers)
    def _(r):
        count[r] = 0

    @pl.loop(0, dest_ref.shape[0])
    def _(i):
        r = dest_ref[i, 0]
        c = jnp.minimum(count[r], CAP - 1)
        table[r * CAP + c] = page_ref[0, i]
        count[r] = c + 1

    def copies(slot, page):
        return [
            pltpu.make_async_copy(source.at[page], out_ref.at[slot, half], sems.at[slot * 2 + half])
            for half, source in enumerate((keys_ref, values_ref))
        ]

    for r in range(peers):
        for c in range(CAP):
            slot = r * CAP + c

            @pl.when(c < count[r])
            def _():
                for copy in copies(slot, table[slot]):
                    copy.start()

            @pl.when(c >= count[r])
            def _():
                out_ref[slot, 0] = jnp.full(out_ref.shape[2:], jnp.inf, out_ref.dtype)
                out_ref[slot, 1] = jnp.zeros(out_ref.shape[2:], out_ref.dtype)

    for r in range(peers):
        for c in range(CAP):
            slot = r * CAP + c

            @pl.when(c < count[r])
            def _():
                for copy in copies(slot, 0):
                    copy.wait()


def pack_pages(dest, pages, cache_keys, cache_values, peers):
    _, page_len, width = cache_keys.shape
    smem = pl.BlockSpec(memory_space=pltpu.SMEM)
    hbm = pl.BlockSpec(memory_space=pltpu.HBM)
    return pl.pallas_call(
        pack_kernel,
        out_shape=jax.ShapeDtypeStruct((peers * CAP, 2, page_len, width), cache_keys.dtype),
        in_specs=[smem, smem, hbm, hbm],
        out_specs=pl.BlockSpec(memory_space=pltpu.VMEM),
        scratch_shapes=[
            pltpu.SMEM((peers * CAP,), jnp.int32),
            pltpu.SMEM((peers,), jnp.int32),
            pltpu.SemaphoreType.DMA((peers * CAP * 2,)),
        ],
        compiler_params=pltpu.CompilerParams(vmem_limit_bytes=PACK_LIMIT),
        cost_estimate=COST,
        name="pack_pages",
    )(dest, pages, cache_keys, cache_values)


def resident_kernel(table_ref, keys_ref, values_ref, out_keys, out_values, sems):
    copies = []
    for j in range(table_ref.shape[0]):
        page = table_ref[j]
        for half, (source, target) in enumerate(((keys_ref, out_keys), (values_ref, out_values))):
            copy = pltpu.make_async_copy(source.at[page], target.at[j], sems.at[j * 2 + half])
            copy.start()
            copies.append(copy)
    for copy in copies:
        copy.wait()


def resident_pages(table, cache_keys, cache_values):
    pages = table.shape[0]
    hbm = pl.BlockSpec(memory_space=pltpu.HBM)
    vmem = pl.BlockSpec(memory_space=pltpu.VMEM)
    shape = jax.ShapeDtypeStruct((pages,) + cache_keys.shape[1:], cache_keys.dtype)
    return pl.pallas_call(
        resident_kernel,
        out_shape=[shape, shape],
        in_specs=[pl.BlockSpec(memory_space=pltpu.SMEM), hbm, hbm],
        out_specs=[vmem, vmem],
        scratch_shapes=[pltpu.SemaphoreType.DMA((pages * 2,))],
        compiler_params=pltpu.CompilerParams(vmem_limit_bytes=PACK_LIMIT),
        cost_estimate=COST,
        name="resident_pages",
    )(table, cache_keys, cache_values)


STAT_ROWS = 16
FACTOR = math.log2(math.e) / math.sqrt(HD)


def head_scores(query, keys):
    return lax.dot_general(keys, query, (((1,), (1,)), ((), ())), preferred_element_type=jnp.float32)


def weigh(scores, row_max, values):
    exponent = jnp.exp2((scores - row_max) * FACTOR)
    mixed = lax.dot_general(
        values, exponent.astype(jnp.bfloat16), (((0,), (0,)), ((), ())), preferred_element_type=jnp.float32
    )
    return mixed, jnp.sum(exponent, axis=0, keepdims=True)


def local_kernel(heads, length_ref, q_ref, rk_ref, rv_ref, k_ref, v_ref, sum_ref, stat_ref):
    resident = rk_ref.shape[0] * rk_ref.shape[1]
    position = lax.broadcasted_iota(jnp.int32, (resident, q_ref.shape[0]), 0)
    for h in range(heads):
        part = slice(h * HD, (h + 1) * HD)
        query = q_ref[:, part]
        values = jnp.concatenate([rv_ref[:, :, part].reshape(-1, HD), v_ref[:, part]], axis=0)
        paged = head_scores(query, rk_ref[:, :, part].reshape(-1, HD))
        paged = jnp.where(position < length_ref[0], paged, -jnp.inf)
        scores = jnp.concatenate([paged, head_scores(query, k_ref[:, part])], axis=0)
        row_max = jnp.max(scores, axis=0, keepdims=True)
        mixed, denominator = weigh(scores, row_max, values)
        sum_ref[part] = mixed
        stat_ref[0, 2 * h : 2 * h + 1] = row_max
        stat_ref[0, 2 * h + 1 : 2 * h + 2] = denominator


def arrived_kernel(heads, usable_ref, q_ref, arrived_ref, sum_ref, stat_ref, out_ref):
    parts = [slice(h * HD, (h + 1) * HD) for h in range(heads)]
    usable = usable_ref[...] > 0
    scores = [head_scores(q_ref[:, part], arrived_ref[:, 0, :, part].reshape(-1, HD)) for part in parts]
    scores = [jnp.where(usable, s, -jnp.inf) for s in scores]
    local_max = [stat_ref[0, 2 * h : 2 * h + 1] for h in range(heads)]
    row_max = [jnp.maximum(m, jnp.max(s, axis=0, keepdims=True)) for m, s in zip(local_max, scores)]
    carry = [jnp.exp2((m - r) * FACTOR) for m, r in zip(local_max, row_max)]
    weighed = [
        weigh(s, r, arrived_ref[:, 1, :, part].reshape(-1, HD)) for s, r, part in zip(scores, row_max, parts)
    ]
    for h, part in enumerate(parts):
        mixed, denominator = weighed[h]
        denominator = denominator + stat_ref[0, 2 * h + 1 : 2 * h + 2] * carry[h]
        mixed = (mixed + sum_ref[part] * carry[h]) / denominator
        out_ref[:, part] = jnp.transpose(mixed).astype(jnp.bfloat16)


def cross_kernel(heads, q_ref, k_ref, v_ref, out_ref):
    for h in range(heads):
        part = slice(h * HD, (h + 1) * HD)
        scores = head_scores(q_ref[:, part], k_ref[:, part])
        mixed, denominator = weigh(scores, jnp.max(scores, axis=0, keepdims=True), v_ref[:, part])
        out_ref[:, part] = jnp.transpose(mixed / denominator).astype(jnp.bfloat16)


def head_group(heads):
    for group in (5, 4, 3, 2):
        if heads % group == 0:
            return group
    return 1


def local_attention(length, query, res_keys, res_values, keys, values):
    tokens, width = query.shape
    group = head_group(width // HD)
    block = group * HD
    steps = width // block
    flat = pl.BlockSpec((tokens, block), lambda h: (0, h))
    paged = pl.BlockSpec(res_keys.shape[:2] + (block,), lambda h: (0, 0, h))
    return pl.pallas_call(
        functools.partial(local_kernel, group),
        out_shape=[
            jax.ShapeDtypeStruct((width, tokens), jnp.float32),
            jax.ShapeDtypeStruct((steps, STAT_ROWS, tokens), jnp.float32),
        ],
        grid=(steps,),
        in_specs=[pl.BlockSpec(memory_space=pltpu.SMEM), flat, paged, paged, flat, flat],
        out_specs=[
            pl.BlockSpec((block, tokens), lambda h: (h, 0)),
            pl.BlockSpec((1, STAT_ROWS, tokens), lambda h: (h, 0, 0)),
        ],
        compiler_params=pltpu.CompilerParams(vmem_limit_bytes=VMEM_LIMIT),
        cost_estimate=COST,
        name="local_attention",
    )(length, query, res_keys, res_values, keys, values)


def arrived_attention(usable, query, arrived, sums, stats):
    tokens, width = query.shape
    steps = stats.shape[0]
    block = width // steps
    flat = pl.BlockSpec((tokens, block), lambda h: (0, h))
    return pl.pallas_call(
        functools.partial(arrived_kernel, block // HD),
        out_shape=jax.ShapeDtypeStruct((tokens, width), query.dtype),
        grid=(steps,),
        in_specs=[
            pl.BlockSpec(usable.shape, lambda h: (0, 0)),
            flat,
            pl.BlockSpec(arrived.shape[:3] + (block,), lambda h: (0, 0, 0, h)),
            pl.BlockSpec((block, tokens), lambda h: (h, 0)),
            pl.BlockSpec((1, STAT_ROWS, tokens), lambda h: (h, 0, 0)),
        ],
        out_specs=flat,
        compiler_params=pltpu.CompilerParams(vmem_limit_bytes=VMEM_LIMIT),
        cost_estimate=COST,
        name="arrived_attention",
    )(usable, query, arrived, sums, stats)


def cross_attention(query, keys, values):
    tokens, width = query.shape
    group = head_group(width // HD)
    block = group * HD
    flat = lambda rows: pl.BlockSpec((rows, block), lambda h: (0, h))
    count = keys.shape[0]
    return pl.pallas_call(
        functools.partial(cross_kernel, group),
        out_shape=jax.ShapeDtypeStruct((tokens, width), query.dtype),
        grid=(width // block,),
        in_specs=[flat(tokens), flat(count), flat(count)],
        out_specs=flat(tokens),
        compiler_params=pltpu.CompilerParams(vmem_limit_bytes=VMEM_LIMIT),
        cost_estimate=COST,
        name="cross_attention",
    )(query, keys, values)


def tp_sum(x):
    if lax.axis_size("tp") == 2:
        return x + lax.ppermute(x, "tp", [(0, 1), (1, 0)])
    return lax.psum(x, "tp")


def after(x, *earlier):
    return lax.optimization_barrier((x,) + earlier)[0]


def swap(x, bits):
    size = lax.axis_size("req")
    return lax.ppermute(x, "req", [(i, i ^ bits) for i in range(size)])


def partial_product(rows, weights):
    return jnp.dot(rows, weights, preferred_element_type=jnp.float32)


def projection_gathered(attended, out_weight):
    width = attended.shape[1]
    weights = lax.all_gather(out_weight, "req", axis=1, tiled=True)
    partial = partial_product(attended, weights).astype(jnp.bfloat16)
    column = lax.axis_index("tp") * width
    if lax.axis_size("tp") == 2:
        other = (lax.axis_size("tp") - 1) * width - column
        own = lax.dynamic_slice_in_dim(partial, column, width, 1)
        sent = lax.dynamic_slice_in_dim(partial, other, width, 1)
        received = lax.ppermute(sent, "tp", [(0, 1), (1, 0)])
        return own.astype(jnp.float32) + received.astype(jnp.float32)
    summed = lax.psum(partial, "tp").astype(jnp.float32)
    return lax.dynamic_slice_in_dim(summed, column, width, 1)


CORE, Y, Z1, Z2 = 1, 2, 4, 8
PIECES = (2, 2, 1)


def planes_weights(out_weight):
    half = out_weight.shape[0] // 2
    core = lax.axis_index("req") % 2
    mine = lax.dynamic_slice_in_dim(out_weight, core * half, half, 0)
    other = lax.dynamic_slice_in_dim(out_weight, (1 - core) * half, half, 0)
    got = swap(other, CORE)
    block = jnp.where(core == 0, jnp.concatenate([mine, got], axis=1), jnp.concatenate([got, mine], axis=1))
    unit = block.shape[1] // sum(PIECES)
    ends = [sum(PIECES[: j + 1]) * unit for j in range(len(PIECES))]
    return block, [lax.slice_in_dim(block, e - p * unit, e, axis=1) for e, p in zip(ends, PIECES)]


def planes_projection(block, block_other, pieces, late_0, arrived, attended):
    half = block.shape[0]
    tokens = attended.shape[0]
    me, x = lax.axis_index("req"), lax.axis_index("tp")
    core, y, z_low, z_high = me % 2, (me // 2) % 2, (me // 4) % 2, me // 8
    own_early = x == z_high

    block_y = after(swap(block, Y), attended)
    late = after(late_0, attended)
    near = swap(attended, Z1)
    rows = jnp.concatenate([attended, near], axis=0)
    rows_mine = jnp.where(core == 0, rows[:, :half], rows[:, half:])
    rows_other = jnp.where(core == 0, rows[:, half:], rows[:, :half])

    def product(w, w_other=None):
        w_other = swap(w, CORE) if w_other is None else w_other
        return (partial_product(rows_mine, w) + partial_product(rows_other, w_other)).astype(jnp.bfloat16)

    early = product(block, block_other), product(block_y)
    own_parts, near_parts = [], []
    first = 0
    for j, piece in enumerate(pieces):
        size = piece.shape[1]
        if j == 1:
            arrival = swap(after(piece, late_0, attended), Z2)
            late = after(arrival, near)
        if j > 1:
            arrival = swap(after(piece, arrival), Z2)
            arrival = late = after(arrival, first_sent)
        late_part = product(jnp.concatenate([late, swap(late, Y)], axis=1))
        if j == 2:
            late_part = after(late_part, sent)
        early_part = jnp.concatenate([e[:, first : first + size] for e in early], axis=1)
        first += size
        kept = jnp.where(own_early, early_part, late_part)
        sent = jnp.where(own_early, late_part, early_part)
        if j == 0:
            first_sent = sent
        received = lax.ppermute(sent, "tp", [(0, 1), (1, 0)])
        total = kept.astype(jnp.float32) + received.astype(jnp.float32)
        own_parts.append(total[:tokens])
        near_parts.append(swap(total[tokens:].astype(jnp.bfloat16), Z1).astype(jnp.float32))

    def ordered(parts):
        this = jnp.concatenate([p[:, : p.shape[1] // 2] for p in parts], axis=1)
        that = jnp.concatenate([p[:, p.shape[1] // 2 :] for p in parts], axis=1)
        return jnp.where(y == 0, jnp.concatenate([this, that], axis=1), jnp.concatenate([that, this], axis=1))

    own, near = ordered(own_parts), ordered(near_parts)
    return jnp.where(z_low == 0, jnp.concatenate([own, near], axis=1), jnp.concatenate([near, own], axis=1))


def shards(
    queries,
    new_keys,
    new_values,
    query_gain,
    key_gain,
    cache_keys,
    cache_values,
    page_table,
    cache_lens,
    mig_pages,
    mig_dest,
    cross_queries,
    text_keys,
    text_values,
    out_weight,
    residual,
    gate,
    shift,
    scale,
):
    tokens, width = queries.shape
    tp, peers = lax.axis_size("tp"), lax.axis_size("req")
    full_width = width * tp
    me = lax.axis_index("req")
    page_len = cache_keys.shape[1]

    packed = pack_pages(mig_dest, mig_pages, cache_keys, cache_values, peers)
    arrived = lax.all_to_all(packed, "req", split_axis=0, concat_axis=0, tiled=True)
    filled = (arrived[:, 0, 0, 0] < jnp.inf).astype(jnp.float32)
    arrived_usable = jnp.broadcast_to(filled[:, None, None], (filled.shape[0], page_len, tokens)).reshape(-1, tokens)

    planes = peers == 16 and tp == 2
    if planes:
        block, pieces = planes_weights(out_weight)
        page_table, cross_queries = after(page_table, block, *pieces), after(cross_queries, block, *pieces)

    query_float = queries.astype(jnp.float32)
    key_float = new_keys.astype(jnp.float32)
    squares = tp_sum(
        jnp.stack([jnp.sum(query_float * query_float, axis=1), jnp.sum(key_float * key_float, axis=1)])
    )
    inverse = lax.rsqrt(squares / full_width + EPS)
    query_normed = (query_float * inverse[0][:, None] * query_gain).astype(jnp.bfloat16)
    key_normed = (key_float * inverse[1][:, None] * key_gain).astype(jnp.bfloat16)

    res_keys, res_values = resident_pages(page_table[0], cache_keys, cache_values)
    sums, stats = local_attention(cache_lens, query_normed, res_keys, res_values, key_normed, new_values)
    cross_out = cross_attention(cross_queries, text_keys, text_values)
    sums = after(sums, cross_out)
    if planes:
        block_other = swap(after(block, sums), CORE)
        late_0 = swap(after(pieces[0], block_other), Z2)
    attended = arrived_attention(arrived_usable, query_normed, arrived, sums, stats)
    if planes:
        projected = planes_projection(block, block_other, pieces, late_0, arrived, attended)
    else:
        projected = projection_gathered(attended, out_weight)

    updated = residual.astype(jnp.float32) + gate.astype(jnp.float32) * projected
    stream = updated.astype(jnp.bfloat16)
    local_mean = jnp.mean(updated, axis=1)
    local_square = jnp.sum(jnp.square(updated - local_mean[:, None]), axis=1)
    if tp == 2:
        theirs = lax.ppermute(jnp.stack([local_mean, local_square]), "tp", [(0, 1), (1, 0)])
        row_mean = (local_mean + theirs[0]) * 0.5
        gap = local_mean - theirs[0]
        row_var = (local_square + theirs[1] + gap * gap * (0.5 * width)) / full_width
    else:
        row_mean = lax.psum(local_mean, "tp") / tp
        offset = local_mean - row_mean
        row_var = lax.psum(local_square + width * offset * offset, "tp") / full_width
    normed = (
        (updated - row_mean[:, None]) * lax.rsqrt(row_var + EPS)[:, None] * (1.0 + scale.astype(jnp.float32))
        + shift.astype(jnp.float32)
    ).astype(jnp.bfloat16)
    return (stream, normed, cross_out)


def solution(mesh):
    in_specs = (
        P("req", "tp"),
        P("req", "tp"),
        P("req", "tp"),
        P("tp"),
        P("tp"),
        P("req", None, "tp"),
        P("req", None, "tp"),
        P("req", None),
        P("req"),
        P("req", None),
        P("req", None),
        P("req", "tp"),
        P("req", "tp"),
        P("req", "tp"),
        P("tp", "req"),
        P("req", "tp"),
        P("req", "tp"),
        P("req", "tp"),
        P("req", "tp"),
    )
    out_specs = (P("req", "tp"), P("req", "tp"), P("req", "tp"))
    return jax.shard_map(shards, mesh=mesh, in_specs=in_specs, out_specs=out_specs, check_vma=False)
```

```python
import functools
import math

import jax
import jax.numpy as jnp
from jax import lax
from jax.experimental import pallas as pl
from jax.experimental.pallas import tpu as pltpu
from jax.sharding import PartitionSpec as P

HD = 128
CAP = 2
EPS = 1e-06
VMEM_LIMIT = 48 * 1024 * 1024
PACK_LIMIT = 60 * 1024 * 1024
COST = pl.CostEstimate(flops=1, bytes_accessed=1, transcendentals=0)


def pack_kernel(dest_ref, page_ref, keys_ref, values_ref, out_ref, table, count, sems):
    peers = count.shape[0]

    @pl.loop(0, peers)
    def _(r):
        count[r] = 0

    @pl.loop(0, dest_ref.shape[0])
    def _(i):
        r = dest_ref[i, 0]
        c = jnp.minimum(count[r], CAP - 1)
        table[r * CAP + c] = page_ref[0, i]
        count[r] = c + 1

    def copies(slot, page):
        return [
            pltpu.make_async_copy(source.at[page], out_ref.at[slot, half], sems.at[slot * 2 + half])
            for half, source in enumerate((keys_ref, values_ref))
        ]

    for r in range(peers):
        for c in range(CAP):
            slot = r * CAP + c

            @pl.when(c < count[r])
            def _():
                for copy in copies(slot, table[slot]):
                    copy.start()

            @pl.when(c >= count[r])
            def _():
                out_ref[slot, 0] = jnp.full(out_ref.shape[2:], jnp.inf, out_ref.dtype)
                out_ref[slot, 1] = jnp.zeros(out_ref.shape[2:], out_ref.dtype)

    for r in range(peers):
        for c in range(CAP):
            slot = r * CAP + c

            @pl.when(c < count[r])
            def _():
                for copy in copies(slot, 0):
                    copy.wait()


def pack_pages(dest, pages, cache_keys, cache_values, peers):
    _, page_len, width = cache_keys.shape
    smem = pl.BlockSpec(memory_space=pltpu.SMEM)
    hbm = pl.BlockSpec(memory_space=pltpu.HBM)
    return pl.pallas_call(
        pack_kernel,
        out_shape=jax.ShapeDtypeStruct((peers * CAP, 2, page_len, width), cache_keys.dtype),
        in_specs=[smem, smem, hbm, hbm],
        out_specs=pl.BlockSpec(memory_space=pltpu.VMEM),
        scratch_shapes=[
            pltpu.SMEM((peers * CAP,), jnp.int32),
            pltpu.SMEM((peers,), jnp.int32),
            pltpu.SemaphoreType.DMA((peers * CAP * 2,)),
        ],
        compiler_params=pltpu.CompilerParams(vmem_limit_bytes=PACK_LIMIT),
        cost_estimate=COST,
        name="pack_pages",
    )(dest, pages, cache_keys, cache_values)


def resident_kernel(table_ref, keys_ref, values_ref, out_keys, out_values, sems):
    copies = []
    for j in range(table_ref.shape[0]):
        page = table_ref[j]
        for half, (source, target) in enumerate(((keys_ref, out_keys), (values_ref, out_values))):
            copy = pltpu.make_async_copy(source.at[page], target.at[j], sems.at[j * 2 + half])
            copy.start()
            copies.append(copy)
    for copy in copies:
        copy.wait()


def resident_pages(table, cache_keys, cache_values):
    pages = table.shape[0]
    hbm = pl.BlockSpec(memory_space=pltpu.HBM)
    vmem = pl.BlockSpec(memory_space=pltpu.VMEM)
    shape = jax.ShapeDtypeStruct((pages,) + cache_keys.shape[1:], cache_keys.dtype)
    return pl.pallas_call(
        resident_kernel,
        out_shape=[shape, shape],
        in_specs=[pl.BlockSpec(memory_space=pltpu.SMEM), hbm, hbm],
        out_specs=[vmem, vmem],
        scratch_shapes=[pltpu.SemaphoreType.DMA((pages * 2,))],
        compiler_params=pltpu.CompilerParams(vmem_limit_bytes=PACK_LIMIT),
        cost_estimate=COST,
        name="resident_pages",
    )(table, cache_keys, cache_values)


STAT_ROWS = 16
FACTOR = math.log2(math.e) / math.sqrt(HD)


def head_scores(query, keys):
    return lax.dot_general(keys, query, (((1,), (1,)), ((), ())), preferred_element_type=jnp.float32)


def weigh(scores, row_max, values):
    exponent = jnp.exp2((scores - row_max) * FACTOR)
    mixed = lax.dot_general(
        values, exponent.astype(jnp.bfloat16), (((0,), (0,)), ((), ())), preferred_element_type=jnp.float32
    )
    return mixed, jnp.sum(exponent, axis=0, keepdims=True)


def local_kernel(heads, length_ref, q_ref, rk_ref, rv_ref, k_ref, v_ref, sum_ref, stat_ref):
    resident = rk_ref.shape[0] * rk_ref.shape[1]
    position = lax.broadcasted_iota(jnp.int32, (resident, q_ref.shape[0]), 0)
    for h in range(heads):
        part = slice(h * HD, (h + 1) * HD)
        query = q_ref[:, part]
        values = jnp.concatenate([rv_ref[:, :, part].reshape(-1, HD), v_ref[:, part]], axis=0)
        paged = head_scores(query, rk_ref[:, :, part].reshape(-1, HD))
        paged = jnp.where(position < length_ref[0], paged, -jnp.inf)
        scores = jnp.concatenate([paged, head_scores(query, k_ref[:, part])], axis=0)
        row_max = jnp.max(scores, axis=0, keepdims=True)
        mixed, denominator = weigh(scores, row_max, values)
        sum_ref[part] = mixed
        stat_ref[0, 2 * h : 2 * h + 1] = row_max
        stat_ref[0, 2 * h + 1 : 2 * h + 2] = denominator


def arrived_kernel(heads, usable_ref, q_ref, arrived_ref, sum_ref, stat_ref, out_ref):
    parts = [slice(h * HD, (h + 1) * HD) for h in range(heads)]
    usable = usable_ref[...] > 0
    scores = [head_scores(q_ref[:, part], arrived_ref[:, 0, :, part].reshape(-1, HD)) for part in parts]
    scores = [jnp.where(usable, s, -jnp.inf) for s in scores]
    local_max = [stat_ref[0, 2 * h : 2 * h + 1] for h in range(heads)]
    row_max = [jnp.maximum(m, jnp.max(s, axis=0, keepdims=True)) for m, s in zip(local_max, scores)]
    carry = [jnp.exp2((m - r) * FACTOR) for m, r in zip(local_max, row_max)]
    weighed = [
        weigh(s, r, arrived_ref[:, 1, :, part].reshape(-1, HD)) for s, r, part in zip(scores, row_max, parts)
    ]
    for h, part in enumerate(parts):
        mixed, denominator = weighed[h]
        denominator = denominator + stat_ref[0, 2 * h + 1 : 2 * h + 2] * carry[h]
        mixed = (mixed + sum_ref[part] * carry[h]) / denominator
        out_ref[:, part] = jnp.transpose(mixed).astype(jnp.bfloat16)


def cross_kernel(heads, q_ref, k_ref, v_ref, out_ref):
    for h in range(heads):
        part = slice(h * HD, (h + 1) * HD)
        scores = head_scores(q_ref[:, part], k_ref[:, part])
        mixed, denominator = weigh(scores, jnp.max(scores, axis=0, keepdims=True), v_ref[:, part])
        out_ref[:, part] = jnp.transpose(mixed / denominator).astype(jnp.bfloat16)


def head_group(heads):
    for group in (5, 4, 3, 2):
        if heads % group == 0:
            return group
    return 1


def local_attention(length, query, res_keys, res_values, keys, values):
    tokens, width = query.shape
    group = head_group(width // HD)
    block = group * HD
    steps = width // block
    flat = pl.BlockSpec((tokens, block), lambda h: (0, h))
    paged = pl.BlockSpec(res_keys.shape[:2] + (block,), lambda h: (0, 0, h))
    return pl.pallas_call(
        functools.partial(local_kernel, group),
        out_shape=[
            jax.ShapeDtypeStruct((width, tokens), jnp.float32),
            jax.ShapeDtypeStruct((steps, STAT_ROWS, tokens), jnp.float32),
        ],
        grid=(steps,),
        in_specs=[pl.BlockSpec(memory_space=pltpu.SMEM), flat, paged, paged, flat, flat],
        out_specs=[
            pl.BlockSpec((block, tokens), lambda h: (h, 0)),
            pl.BlockSpec((1, STAT_ROWS, tokens), lambda h: (h, 0, 0)),
        ],
        compiler_params=pltpu.CompilerParams(vmem_limit_bytes=VMEM_LIMIT),
        cost_estimate=COST,
        name="local_attention",
    )(length, query, res_keys, res_values, keys, values)


def arrived_attention(usable, query, arrived, sums, stats):
    tokens, width = query.shape
    steps = stats.shape[0]
    block = width // steps
    flat = pl.BlockSpec((tokens, block), lambda h: (0, h))
    return pl.pallas_call(
        functools.partial(arrived_kernel, block // HD),
        out_shape=jax.ShapeDtypeStruct((tokens, width), query.dtype),
        grid=(steps,),
        in_specs=[
            pl.BlockSpec(usable.shape, lambda h: (0, 0)),
            flat,
            pl.BlockSpec(arrived.shape[:3] + (block,), lambda h: (0, 0, 0, h)),
            pl.BlockSpec((block, tokens), lambda h: (h, 0)),
            pl.BlockSpec((1, STAT_ROWS, tokens), lambda h: (h, 0, 0)),
        ],
        out_specs=flat,
        compiler_params=pltpu.CompilerParams(vmem_limit_bytes=VMEM_LIMIT),
        cost_estimate=COST,
        name="arrived_attention",
    )(usable, query, arrived, sums, stats)


def cross_attention(query, keys, values):
    tokens, width = query.shape
    group = head_group(width // HD)
    block = group * HD
    flat = lambda rows: pl.BlockSpec((rows, block), lambda h: (0, h))
    count = keys.shape[0]
    return pl.pallas_call(
        functools.partial(cross_kernel, group),
        out_shape=jax.ShapeDtypeStruct((tokens, width), query.dtype),
        grid=(width // block,),
        in_specs=[flat(tokens), flat(count), flat(count)],
        out_specs=flat(tokens),
        compiler_params=pltpu.CompilerParams(vmem_limit_bytes=VMEM_LIMIT),
        cost_estimate=COST,
        name="cross_attention",
    )(query, keys, values)


def tp_sum(x):
    if lax.axis_size("tp") == 2:
        return x + lax.ppermute(x, "tp", [(0, 1), (1, 0)])
    return lax.psum(x, "tp")


def after(x, *earlier):
    return lax.optimization_barrier((x,) + earlier)[0]


def swap(x, bits):
    size = lax.axis_size("req")
    return lax.ppermute(x, "req", [(i, i ^ bits) for i in range(size)])


def partial_product(rows, weights):
    return jnp.dot(rows, weights, preferred_element_type=jnp.float32)


def projection_gathered(attended, out_weight):
    width = attended.shape[1]
    weights = lax.all_gather(out_weight, "req", axis=1, tiled=True)
    partial = partial_product(attended, weights).astype(jnp.bfloat16)
    column = lax.axis_index("tp") * width
    if lax.axis_size("tp") == 2:
        other = (lax.axis_size("tp") - 1) * width - column
        own = lax.dynamic_slice_in_dim(partial, column, width, 1)
        sent = lax.dynamic_slice_in_dim(partial, other, width, 1)
        received = lax.ppermute(sent, "tp", [(0, 1), (1, 0)])
        return own.astype(jnp.float32) + received.astype(jnp.float32)
    summed = lax.psum(partial, "tp").astype(jnp.float32)
    return lax.dynamic_slice_in_dim(summed, column, width, 1)


CORE, Y, Z1, Z2 = 1, 2, 4, 8
PIECES = (2, 2, 1)


def planes_weights(out_weight):
    half = out_weight.shape[0] // 2
    core = lax.axis_index("req") % 2
    mine = lax.dynamic_slice_in_dim(out_weight, core * half, half, 0)
    other = lax.dynamic_slice_in_dim(out_weight, (1 - core) * half, half, 0)
    got = swap(other, CORE)
    block = jnp.where(core == 0, jnp.concatenate([mine, got], axis=1), jnp.concatenate([got, mine], axis=1))
    unit = block.shape[1] // sum(PIECES)
    ends = [sum(PIECES[: j + 1]) * unit for j in range(len(PIECES))]
    return block, [lax.slice_in_dim(block, e - p * unit, e, axis=1) for e, p in zip(ends, PIECES)]


def planes_projection(block, block_other, pieces, late_0, arrived, attended):
    half = block.shape[0]
    tokens = attended.shape[0]
    me, x = lax.axis_index("req"), lax.axis_index("tp")
    core, y, z_low, z_high = me % 2, (me // 2) % 2, (me // 4) % 2, me // 8
    own_early = x == z_high

    block_y = after(swap(block, Y), attended)
    late = after(late_0, attended)
    near = swap(attended, Z1)
    rows = jnp.concatenate([attended, near], axis=0)
    rows_mine = jnp.where(core == 0, rows[:, :half], rows[:, half:])
    rows_other = jnp.where(core == 0, rows[:, half:], rows[:, :half])

    def product(w, w_other=None):
        w_other = swap(w, CORE) if w_other is None else w_other
        return (partial_product(rows_mine, w) + partial_product(rows_other, w_other)).astype(jnp.bfloat16)

    early = product(block, block_other), product(block_y)
    own_parts, near_parts = [], []
    first = 0
    for j, piece in enumerate(pieces):
        size = piece.shape[1]
        if j == 1:
            arrival = swap(after(piece, late_0, attended), Z2)
            late = after(arrival, near)
        if j > 1:
            arrival = swap(after(piece, arrival), Z2)
            arrival = late = after(arrival, first_sent)
        late_part = product(jnp.concatenate([late, swap(late, Y)], axis=1))
        if j == 2:
            late_part = after(late_part, sent)
        early_part = jnp.concatenate([e[:, first : first + size] for e in early], axis=1)
        first += size
        kept = jnp.where(own_early, early_part, late_part)
        sent = jnp.where(own_early, late_part, early_part)
        if j == 0:
            first_sent = sent
        if j == 1:
            near_sum, own_sum = [
                kept[part].astype(jnp.float32)
                + lax.ppermute(sent[part], "tp", [(0, 1), (1, 0)]).astype(jnp.float32)
                for part in (slice(tokens, None), slice(0, tokens))
            ]
        else:
            total = kept.astype(jnp.float32) + lax.ppermute(sent, "tp", [(0, 1), (1, 0)]).astype(jnp.float32)
            own_sum, near_sum = total[:tokens], total[tokens:]
        own_parts.append(own_sum)
        near_parts.append(swap(near_sum.astype(jnp.bfloat16), Z1).astype(jnp.float32))

    def ordered(parts):
        this = jnp.concatenate([p[:, : p.shape[1] // 2] for p in parts], axis=1)
        that = jnp.concatenate([p[:, p.shape[1] // 2 :] for p in parts], axis=1)
        return jnp.where(y == 0, jnp.concatenate([this, that], axis=1), jnp.concatenate([that, this], axis=1))

    own, near = ordered(own_parts), ordered(near_parts)
    return jnp.where(z_low == 0, jnp.concatenate([own, near], axis=1), jnp.concatenate([near, own], axis=1))


def shards(
    queries,
    new_keys,
    new_values,
    query_gain,
    key_gain,
    cache_keys,
    cache_values,
    page_table,
    cache_lens,
    mig_pages,
    mig_dest,
    cross_queries,
    text_keys,
    text_values,
    out_weight,
    residual,
    gate,
    shift,
    scale,
):
    tokens, width = queries.shape
    tp, peers = lax.axis_size("tp"), lax.axis_size("req")
    full_width = width * tp
    me = lax.axis_index("req")
    page_len = cache_keys.shape[1]

    packed = pack_pages(mig_dest, mig_pages, cache_keys, cache_values, peers)
    arrived = lax.all_to_all(packed, "req", split_axis=0, concat_axis=0, tiled=True)
    filled = (arrived[:, 0, 0, 0] < jnp.inf).astype(jnp.float32)
    arrived_usable = jnp.broadcast_to(filled[:, None, None], (filled.shape[0], page_len, tokens)).reshape(-1, tokens)

    planes = peers == 16 and tp == 2
    if planes:
        block, pieces = planes_weights(out_weight)
        page_table, cross_queries = after(page_table, block, *pieces), after(cross_queries, block, *pieces)

    query_float = queries.astype(jnp.float32)
    key_float = new_keys.astype(jnp.float32)
    squares = tp_sum(
        jnp.stack([jnp.sum(query_float * query_float, axis=1), jnp.sum(key_float * key_float, axis=1)])
    )
    inverse = lax.rsqrt(squares / full_width + EPS)
    query_normed = (query_float * inverse[0][:, None] * query_gain).astype(jnp.bfloat16)
    key_normed = (key_float * inverse[1][:, None] * key_gain).astype(jnp.bfloat16)

    res_keys, res_values = resident_pages(page_table[0], cache_keys, cache_values)
    sums, stats = local_attention(cache_lens, query_normed, res_keys, res_values, key_normed, new_values)
    cross_out = cross_attention(cross_queries, text_keys, text_values)
    sums = after(sums, cross_out)
    if planes:
        block_other = swap(after(block, sums), CORE)
        late_0 = swap(after(pieces[0], block_other), Z2)
    attended = arrived_attention(arrived_usable, query_normed, arrived, sums, stats)
    if planes:
        projected = planes_projection(block, block_other, pieces, late_0, arrived, attended)
    else:
        projected = projection_gathered(attended, out_weight)

    updated = residual.astype(jnp.float32) + gate.astype(jnp.float32) * projected
    stream = updated.astype(jnp.bfloat16)
    local_mean = jnp.mean(updated, axis=1)
    local_square = jnp.sum(jnp.square(updated - local_mean[:, None]), axis=1)
    if tp == 2:
        theirs = lax.ppermute(jnp.stack([local_mean, local_square]), "tp", [(0, 1), (1, 0)])
        row_mean = (local_mean + theirs[0]) * 0.5
        gap = local_mean - theirs[0]
        row_var = (local_square + theirs[1] + gap * gap * (0.5 * width)) / full_width
    else:
        row_mean = lax.psum(local_mean, "tp") / tp
        offset = local_mean - row_mean
        row_var = lax.psum(local_square + width * offset * offset, "tp") / full_width
    normed = (
        (updated - row_mean[:, None]) * lax.rsqrt(row_var + EPS)[:, None] * (1.0 + scale.astype(jnp.float32))
        + shift.astype(jnp.float32)
    ).astype(jnp.bfloat16)
    return (stream, normed, cross_out)


def solution(mesh):
    in_specs = (
        P("req", "tp"),
        P("req", "tp"),
        P("req", "tp"),
        P("tp"),
        P("tp"),
        P("req", None, "tp"),
        P("req", None, "tp"),
        P("req", None),
        P("req"),
        P("req", None),
        P("req", None),
        P("req", "tp"),
        P("req", "tp"),
        P("req", "tp"),
        P("tp", "req"),
        P("req", "tp"),
        P("req", "tp"),
        P("req", "tp"),
        P("req", "tp"),
    )
    out_specs = (P("req", "tp"), P("req", "tp"), P("req", "tp"))
    return jax.shard_map(shards, mesh=mesh, in_specs=in_specs, out_specs=out_specs, check_vma=False)
```
